32 devices in a mesh: gy: 4 (over y, x), gz: 8 (over z, core).
Axes of the slice: x: 2, y: 2, z: 4, core: 2. Of those that a mesh axis runs over, the one named last changes fastest.
Arguments:
- density: float32 [1024, 128, 256], P('gy', 'gz'), may hold values from 0.5 to 2
- momentum: float32 [3, 1024, 128, 256], P(None, 'gy', 'gz'), may hold values from -3 to 3
- energy: float32 [1024, 128, 256], P('gy', 'gz'), may hold values from 2 to 4
- wall_operator: float32 [1024, 1024], replicated, may hold values from -0.1875 to 0.1875
- span_operator: float32 [128, 128], replicated, may hold values from -0.5 to 0.5
- damping: float32 [1024], replicated, may hold values from 0.1 to 1
Outputs:
- new_density: float32 [1024, 128, 256], P('gy', 'gz')
- new_momentum: float32 [3, 1024, 128, 256], P(None, 'gy', 'gz')
- new_energy: float32 [1024, 128, 256], P('gy', 'gz')
The draws below stay inside these ranges and needn't reach their ends.
All inputs are finite; a program needn't handle non-finite values.
Results may differ from the reference program's by a relative error of at most 0.00009.
Values sent between devices are 32-bit elements; how exact they have to be, the bound alone decides.
No kernel may reach another device: no remote copies, remote signals or barrier semaphores. Data moves between devices by JAX's collectives and lax.ppermute only.
A program may use at most 320 MiB of HBM per device.

```python
import math
import jax
import jax.numpy as jnp
from jax import lax

NY = 1024
NZ = 128
NX = 256


def block_levels(key, dims, shards, smallest, high):
    level = 1.0
    for position, blocks in shards:
        heights = jax.random.uniform(jax.random.fold_in(jax.random.fold_in(key, 6), position), (blocks,), jnp.float32, smallest / len(shards), high / len(shards))
        level = level * jnp.repeat(jnp.exp(heights), dims[position] // blocks).reshape((-1,) + (1,) * (len(dims) - 1 - position))
    return level


def centred(own_key, shape, spread, bound, cuts=(), dtype=jnp.bfloat16):
    array = jax.random.normal(own_key, shape, jnp.float32) * spread
    if len(cuts) > 0:
        array = block_levels(own_key, shape, cuts, -0.22, 0.18) * array
    return jnp.clip(array, min=-bound, max=bound).astype(dtype)


def setup_inputs(seed: int = 0) -> dict:
    seeds = jax.random.split(jax.random.key(seed), 7)
    density = jnp.clip(0.5 + 1.5 * jax.random.uniform(seeds[0], (NY, NZ, NX), jnp.float32) ** block_levels(seeds[0], (NY, NZ, NX), ((0, 4), (1, 8)), -0.2, 0.2), 0.5, 2.0)
    momentum = centred(seeds[1], (3, NY, NZ, NX), 0.7, 3.0, ((1, 4), (2, 8)), jnp.float32)
    energy = jnp.clip(2.0 + 2.0 * jax.random.uniform(seeds[2], (NY, NZ, NX), jnp.float32) ** block_levels(seeds[2], (NY, NZ, NX), ((0, 4), (1, 8)), -0.2, 0.2), 2.0, 4.0)
    wall_operator = centred(seeds[3], (NY, NY), NY ** -0.5, 0.1875, (), jnp.float32)
    span_operator = centred(seeds[4], (NZ, NZ), NZ ** -0.5, 0.5, (), jnp.float32)
    damping = jnp.clip(jnp.exp(jax.random.uniform(seeds[5], (NY,), jnp.float32, math.log(0.1), math.log(1.0))), 0.1, 1.0)
    return dict(density=density, momentum=momentum, energy=energy, wall_operator=wall_operator, span_operator=span_operator, damping=damping)


gamma_less = 0.4
time_step = 0.1


def flux_along(conserved, direction):
    velocity = conserved[1 + direction] / conserved[0]
    kinetic = 0.5 * (conserved[1] * conserved[1] + conserved[2] * conserved[2] + conserved[3] * conserved[3]) / conserved[0]
    pressure = gamma_less * (conserved[4] - kinetic)
    components = [conserved[1 + direction]]
    for column in range(3):
        product = conserved[1 + column] * velocity
        if column == direction:
            product = product + pressure
        components.append(product)
    components.append((conserved[4] + pressure) * velocity)
    return jnp.stack(components)


def x_derivative(flux_field):
    widths = [(0, 0)] * (flux_field.ndim - 1) + [(2, 2)]
    padded = jnp.pad(flux_field, widths, mode="edge")
    return (8.0 * (padded[..., 3:-1] - padded[..., 1:-3]) - (padded[..., 4:] - padded[..., :-4])) / 12.0


def fourth_difference(padded, along_axis, length_out):
    def shifted(offset):
        return lax.slice_in_dim(padded, offset, offset + length_out, axis=along_axis)
    return shifted(0) - 4.0 * shifted(1) + 6.0 * shifted(2) - 4.0 * shifted(3) + shifted(4)


def reference(density, momentum, energy, wall_operator, span_operator, damping):
    conserved = jnp.concatenate([density[None], momentum, energy[None]], axis=0)

    def plane_part(one_plane):
        across = flux_along(one_plane, 0)
        upward = flux_along(one_plane, 1)
        deriv_y = jnp.einsum("ij,fjx->fix", wall_operator, upward, precision=lax.Precision.HIGHEST)
        padded = jnp.pad(one_plane, ((0, 0), (2, 2), (0, 0)))
        return -x_derivative(across) - deriv_y - damping[None, :, None] * fourth_difference(padded, 1, NY)

    planes = lax.map(plane_part, jnp.moveaxis(conserved, 2, 0))
    plane_terms = jnp.moveaxis(planes, 0, 2)

    def row_part(inputs):
        one_row, weight = inputs
        sideways = flux_along(one_row, 2)
        deriv_z = jnp.einsum("ij,fjx->fix", span_operator, sideways, precision=lax.Precision.HIGHEST)
        padded = jnp.concatenate([one_row[:, -2:], one_row, one_row[:, :2]], axis=1)
        return -deriv_z - weight * fourth_difference(padded, 1, NZ)

    rows_out = lax.map(row_part, (jnp.moveaxis(conserved, 1, 0), damping))
    row_terms = jnp.moveaxis(rows_out, 0, 1)
    advanced = conserved + time_step * (plane_terms + row_terms)
    return advanced[0], advanced[1:4], advanced[4]
```

```python
import functools

import jax
import jax.numpy as jnp
from jax import lax
from jax.experimental import pallas as pl
from jax.experimental.pallas import tpu as pltpu
from jax.sharding import PartitionSpec as P

gamma_less = 0.4
time_step = 0.1
vmem_bytes = 56 * 1024 * 1024


def divisor_up_to(number, limit):
    return max(d for d in range(1, limit + 1) if number % d == 0)


def hop(index, step, size, sign):
    if size & (size - 1) == 0:
        return index ^ step
    return (index + sign * step) % size


def fluxes(fields, direction):
    density, momentum, energy = fields[0], fields[1:4], fields[4]
    inverse = 1.0 / density
    velocity = momentum[direction] * inverse
    square = momentum[0] * momentum[0] + momentum[1] * momentum[1] + momentum[2] * momentum[2]
    pressure = gamma_less * (energy - 0.5 * square * inverse)
    out = [momentum[direction]]
    for column in range(3):
        product = momentum[column] * velocity
        if column == direction:
            product = product + pressure
        out.append(product)
    out.append((energy + pressure) * velocity)
    return out


def halves(value):
    high = value.astype(jnp.bfloat16)
    low = (value - high.astype(jnp.float32)).astype(jnp.bfloat16)
    return high, low


def split_outside(value):
    high = lax.reduce_precision(value, exponent_bits=8, mantissa_bits=7)
    return high.astype(jnp.bfloat16), (value - high).astype(jnp.bfloat16)


def dot(a, b):
    return jnp.dot(a, b, preferred_element_type=jnp.float32)


def call(body, name, order, operands, grid, in_specs, out_specs, out_shape, scratch=(), aliases=None, flops=0):
    scalars = tuple(order)
    moved = sum(4 * o.size for o in operands) + sum(4 * o.size for o in out_shape)
    return pl.pallas_call(
        body,
        name=name,
        grid_spec=pltpu.PrefetchScalarGridSpec(
            num_scalar_prefetch=len(scalars),
            grid=grid,
            in_specs=in_specs,
            out_specs=out_specs,
            scratch_shapes=list(scratch),
        ),
        out_shape=out_shape,
        input_output_aliases={} if aliases is None else aliases,
        compiler_params=pltpu.CompilerParams(vmem_limit_bytes=vmem_bytes),
        cost_estimate=pl.CostEstimate(flops=flops, bytes_accessed=moved, transcendentals=0),
    )(*scalars, *operands)


def pack_span_kernel(order, density, momentum, energy, *pieces):
    for k, piece in enumerate(pieces):
        block = order[k]
        piece[0] = density[block]
        for column in range(3):
            piece[1 + column] = momentum[column, block]
        piece[4] = energy[block]


def pack_span(blocks, chunk, chunks, density, momentum, energy):
    n, share, zl, nx = density.shape
    rows = share // chunks
    r = divisor_up_to(rows, 2)
    first = chunk * (rows // r)
    flat = pl.BlockSpec((n, r, zl, nx), lambda i, s: (0, first + i, 0, 0))
    return call(
        pack_span_kernel,
        f"pack_span_{chunk}",
        (blocks,),
        (density, momentum, energy),
        (rows // r,),
        [flat, pl.BlockSpec((3, n, r, zl, nx), lambda i, s: (0, 0, first + i, 0, 0)), flat],
        [pl.BlockSpec((5, r, zl, nx), lambda i, s: (0, i, 0, 0))] * n,
        [jax.ShapeDtypeStruct((5, rows, zl, nx), jnp.float32)] * n,
    )


def span_kernel(n, weights, both, *refs):
    pieces, outs = refs[:n], refs[n:]
    _, r, zl, nx = pieces[0].shape
    nz = n * zl

    @pl.loop(0, r)
    def _(row):
        weight = weights[pl.program_id(0) * r + row]
        fields = [jnp.concatenate([p[f, row] for p in pieces], axis=0) for f in range(5)]
        for f, flux in enumerate(fluxes(fields, 2)):
            high, low = halves(jnp.concatenate([flux, weight * fields[f]], axis=0))
            total = dot(both[...], high)
            total = total[:nz] + total[nz:] + dot(both[:nz], low)
            for k, out in enumerate(outs):
                out[f, row] = total[k * zl : (k + 1) * zl]


def span_terms(chunk, weights, both, pieces):
    n = len(pieces)
    _, rows, zl, nx = pieces[0].shape
    r = divisor_up_to(rows, 2)
    nz = n * zl
    spec = pl.BlockSpec((5, r, zl, nx), lambda i, s: (0, i, 0, 0))
    return call(
        functools.partial(span_kernel, n),
        f"span_terms_{chunk}",
        (weights,),
        (both, *pieces),
        (rows // r,),
        [pl.BlockSpec(both.shape, lambda i, s: (0, 0))] + [spec] * n,
        [spec] * n,
        [jax.ShapeDtypeStruct(p.shape, jnp.float32) for p in pieces],
        flops=5 * rows * 6 * nz * 2 * nz * nx,
    )


def pack_wall_kernel(zl, order, density, momentum, energy, *refs):
    pieces, narrow = refs[:-1], refs[-1]
    _, zz, rows, nx = pieces[0].shape
    lane = narrow.shape[-1]
    for half in range(nx // lane):
        lanes = slice(half * lane, (half + 1) * lane)
        narrow[half, 0] = density[:, lanes]
        for column in range(3):
            narrow[half, 1 + column] = momentum[column, :, lanes]
        narrow[half, 4] = energy[:, lanes]
    for k, piece in enumerate(pieces):
        for z in range(zz):
            lines = pl.ds(order[k] * zz + z, rows, stride=zl)
            for half in range(nx // lane):
                lanes = slice(half * lane, (half + 1) * lane)
                for f in range(5):
                    piece[f, z, :, lanes] = narrow[half, f, lines, :]


def pack_wall(blocks, density, momentum, energy):
    m = blocks.shape[0]
    jl, zl, nx = density.shape
    zz = zl // m
    lane = divisor_up_to(nx, 128)
    rows = divisor_up_to(jl, 32)
    flat = pl.BlockSpec((rows * zl, nx), lambda i, s: (i, 0))
    return call(
        functools.partial(pack_wall_kernel, zl),
        "pack_wall",
        (blocks,),
        (density.reshape(jl * zl, nx), momentum.reshape(3, jl * zl, nx), energy.reshape(jl * zl, nx)),
        (jl // rows,),
        [flat, pl.BlockSpec((3, rows * zl, nx), lambda i, s: (0, i, 0)), flat],
        [pl.BlockSpec((5, zz, rows, nx), lambda i, s: (0, 0, i, 0))] * m,
        [jax.ShapeDtypeStruct((5, zz, jl, nx), jnp.float32)] * m,
        scratch=[pltpu.VMEM((nx // lane, 5, rows * zl, lane), jnp.float32)],
    )


def wall_kernel(m, order, high, low, damping, *refs):
    pieces, outs = refs[:m], refs[m : 2 * m]
    kept, flux_high, flux_low = refs[2 * m :]
    jl, nx = pieces[0].shape[2:]
    ny = m * jl
    step = divisor_up_to(jl, 32)
    for f in range(5):
        kept[f, 0:8] = jnp.zeros((8, nx), jnp.float32)
        kept[f, 8 + ny : 16 + ny] = jnp.zeros((8, nx), jnp.float32)
    for k in range(m):

        @pl.loop(0, jl // step)
        def _(i):
            here = pl.ds(pl.multiple_of(i * step, step), step)
            there = pl.multiple_of(order[k] * jl + i * step, step)
            fields = [pieces[k][f, 0, here, :] for f in range(5)]
            for f, flux in enumerate(fluxes(fields, 1)):
                kept[f, pl.ds(there + 8, step), :] = fields[f]
                flux_high[f, pl.ds(there, step), :], flux_low[f, pl.ds(there, step), :] = halves(flux)

    for k in range(m):
        first = pl.multiple_of(order[k] * jl, jl)
        rows = pl.ds(first, jl)

        @pl.loop(0, 5)
        def _(f):
            total = dot(high[rows, :], flux_high[f]) + dot(low[rows, :], flux_high[f])
            outs[k][f, 0] = total + dot(high[rows, :], flux_low[f])
            part = divisor_up_to(jl, 64)

            @pl.loop(0, jl // part)
            def _(i):
                at = pl.multiple_of(i * part, part)
                c = kept[f, pl.ds(first + at, part + 16), :]

                def shifted(offset):
                    return c[8 + offset : 8 + offset + part]

                fourth = (
                    shifted(-2) - 4.0 * shifted(-1) + 6.0 * shifted(0) - 4.0 * shifted(1) + shifted(2)
                )
                weight = damping[pl.ds(first + at, part), :]
                outs[k][f, 0, pl.ds(at, part), :] += weight * fourth


def wall_terms(blocks, operator, damping, pieces):
    m = len(pieces)
    _, zz, jl, nx = pieces[0].shape
    ny = m * jl
    high, low = split_outside(operator)
    spec = pl.BlockSpec((5, 1, jl, nx), lambda i, s: (0, i, 0, 0))
    whole = pl.BlockSpec((ny, ny), lambda i, s: (0, 0))
    return call(
        functools.partial(wall_kernel, m),
        "wall_terms",
        (blocks,),
        (high, low, damping.reshape(ny, 1), *pieces),
        (zz,),
        [whole, whole, pl.BlockSpec((ny, 1), lambda i, s: (0, 0))] + [spec] * m,
        [spec] * m,
        [jax.ShapeDtypeStruct(p.shape, jnp.float32) for p in pieces],
        scratch=[
            pltpu.VMEM((5, ny + 16, nx), jnp.float32),
            pltpu.VMEM((5, ny, nx), jnp.bfloat16),
            pltpu.VMEM((5, ny, nx), jnp.bfloat16),
        ],
        flops=6 * 5 * zz * ny * ny * nx,
    )


def base_kernel(m, zl, order, density, momentum, energy, *refs):
    pieces, outs, wall = refs[:m], refs[m : m + 3], refs[m + 3]
    _, zz, rows, nx = pieces[0].shape
    lane = wall.shape[-1]
    for k, piece in enumerate(pieces):
        for z in range(zz):
            lines = pl.ds(order[k] * zz + z, rows, stride=zl)
            for half in range(nx // lane):
                lanes = slice(half * lane, (half + 1) * lane)
                for f in range(5):
                    wall[half, f, lines, :] = piece[f, z, :, lanes]
    part = 16

    @pl.loop(0, rows * zl // part)
    def _(i):
        here = pl.ds(pl.multiple_of(i * part, part), part)
        fields = [density[here, :]] + [momentum[column, here, :] for column in range(3)] + [energy[here, :]]
        column = lax.broadcasted_iota(jnp.int32, (part, nx), 1)
        for f, flux in enumerate(fluxes(fields, 0)):
            first, last = flux[:, :1], flux[:, nx - 1 :]
            above1 = jnp.where(column >= nx - 1, last, pltpu.roll(flux, nx - 1, 1))
            above2 = jnp.where(column >= nx - 2, last, pltpu.roll(flux, nx - 2, 1))
            below1 = jnp.where(column < 1, first, pltpu.roll(flux, 1, 1))
            below2 = jnp.where(column < 2, first, pltpu.roll(flux, 2, 1))
            along = (8.0 * (above1 - below1) - (above2 - below2)) * (1.0 / 12.0)
            across = jnp.concatenate([wall[half, f, here, :] for half in range(wall.shape[0])], axis=1)
            value = fields[f] - time_step * (along + across)
            if f == 0:
                outs[0][here, :] = value
            elif f == 4:
                outs[2][here, :] = value
            else:
                outs[1][f - 1, here, :] = value


def base_fields(blocks, density, momentum, energy, pieces):
    m = len(pieces)
    jl, zl, nx = density.shape
    zz = zl // m
    lane = divisor_up_to(nx, 128)
    rows = divisor_up_to(jl, 16)
    flat = pl.BlockSpec((rows * zl, nx), lambda i, s: (i, 0))
    three = pl.BlockSpec((3, rows * zl, nx), lambda i, s: (0, i, 0))
    shape = jax.ShapeDtypeStruct((jl * zl, nx), jnp.float32)
    outs = call(
        functools.partial(base_kernel, m, zl),
        "base_fields",
        (blocks,),
        (density.reshape(jl * zl, nx), momentum.reshape(3, jl * zl, nx), energy.reshape(jl * zl, nx), *pieces),
        (jl // rows,),
        [flat, three, flat] + [pl.BlockSpec((5, zz, rows, nx), lambda i, s: (0, 0, i, 0))] * m,
        [flat, three, flat],
        [shape, jax.ShapeDtypeStruct((3, jl * zl, nx), jnp.float32), shape],
        scratch=[pltpu.VMEM((nx // lane, 5, rows * zl, lane), jnp.float32)],
    )
    return outs


def add_span_kernel(n, order, density, momentum, energy, *refs):
    pieces, outs = refs[:n], refs[n:]
    for k, piece in enumerate(pieces):
        block = order[k]
        outs[0][block] = density[block] - time_step * piece[0]
        for column in range(3):
            outs[1][column, block] = momentum[column, block] - time_step * piece[1 + column]
        outs[2][block] = energy[block] - time_step * piece[4]


def add_span(blocks, chunk, chunks, fields, pieces):
    n = len(pieces)
    share, zl, nx = fields[0].shape[1:]
    rows = share // chunks
    r = divisor_up_to(rows, 2)
    first = chunk * (rows // r)
    flat = pl.BlockSpec((n, r, zl, nx), lambda i, s: (0, first + i, 0, 0))
    three = pl.BlockSpec((3, n, r, zl, nx), lambda i, s: (0, 0, first + i, 0, 0))
    return call(
        functools.partial(add_span_kernel, n),
        f"add_span_{chunk}",
        (blocks,),
        (*fields, *pieces),
        (rows // r,),
        [flat, three, flat] + [pl.BlockSpec((5, r, zl, nx), lambda i, s: (0, i, 0, 0))] * n,
        [flat, three, flat],
        [jax.ShapeDtypeStruct(f.shape, f.dtype) for f in fields],
        aliases={1: 0, 2: 1, 3: 2},
    )


def exchange(pieces, axis, sign, sequence):
    size = len(pieces)
    out = list(pieces)
    for k in sequence:
        pairs = [(i, hop(i, k, size, sign)) for i in range(size)]
        out[k] = lax.ppermute(pieces[k], axis, pairs)
    return out


def local(density, momentum, energy, wall_operator, span_operator, damping, *, chunks):
    jl, zl, nx = density.shape
    nz = span_operator.shape[0]
    m, n = lax.axis_size("gy"), lax.axis_size("gz")
    gy, gz = lax.axis_index("gy"), lax.axis_index("gz")
    share = jl // n
    chunks = divisor_up_to(share, chunks)
    rows = share // chunks

    span_to = jnp.stack([jnp.asarray(hop(gz, k, n, 1), jnp.int32) for k in range(n)])
    span_from = jnp.stack([jnp.asarray(hop(gz, k, n, -1), jnp.int32) for k in range(n)])
    wall_to = jnp.stack([jnp.asarray(hop(gy, k, m, 1), jnp.int32) for k in range(m)])
    wall_from = jnp.stack([jnp.asarray(hop(gy, k, m, -1), jnp.int32) for k in range(m)])

    by_share = (
        density.reshape(n, share, zl, nx),
        momentum.reshape(3, n, share, zl, nx),
        energy.reshape(n, share, zl, nx),
    )
    far_first = range(n - 1, 0, -1)
    span_out = [
        exchange(pack_span(span_to, c, chunks, *by_share), "gz", 1, far_first) for c in range(chunks)
    ]
    wall_out = exchange(pack_wall(wall_to, density, momentum, energy), "gy", 1, range(m - 1, 0, -1))

    identity = jnp.eye(nz, dtype=jnp.float32)
    fourth = 6.0 * identity
    for offset, factor in ((1, -4.0), (-1, -4.0), (2, 1.0), (-2, 1.0)):
        fourth = fourth + factor * jnp.roll(identity, offset, 1)

    def in_order_of_arrival(matrix):
        blocks = matrix.reshape(n, zl, n, zl)
        blocks = jnp.take(jnp.take(blocks, span_from, axis=0), span_from, axis=2)
        return blocks.reshape(nz, nz)

    both = jnp.concatenate([in_order_of_arrival(span_operator), in_order_of_arrival(fourth)], axis=1)
    both = jnp.concatenate(split_outside(both), axis=0)

    wall_back = exchange(wall_terms(wall_from, wall_operator, damping, wall_out), "gy", -1, range(m - 1, 0, -1))
    span_back = []
    for c in range(chunks):
        weights = lax.dynamic_slice_in_dim(damping, gy * jl + gz * share + c * rows, rows)
        span_back.append(exchange(span_terms(c, weights, both, span_out[c]), "gz", -1, far_first))

    fields = base_fields(wall_to, density, momentum, energy, wall_back)
    fields = (
        fields[0].reshape(n, share, zl, nx),
        fields[1].reshape(3, n, share, zl, nx),
        fields[2].reshape(n, share, zl, nx),
    )
    for c in range(chunks):
        fields = add_span(span_to, c, chunks, fields, span_back[c])
    return (
        fields[0].reshape(jl, zl, nx),
        fields[1].reshape(3, jl, zl, nx),
        fields[2].reshape(jl, zl, nx),
    )


def solution(mesh):
    in_specs = (P("gy", "gz", None), P(None, "gy", "gz", None), P("gy", "gz", None), P(), P(), P())
    out_specs = (P("gy", "gz", None), P(None, "gy", "gz", None), P("gy", "gz", None))
    return jax.shard_map(
        functools.partial(local, chunks=2), mesh=mesh, in_specs=in_specs, out_specs=out_specs, check_vma=False
    )
```

```python
import functools

import jax
import jax.numpy as jnp
from jax import lax
from jax.experimental import pallas as pl
from jax.experimental.pallas import tpu as pltpu
from jax.sharding import PartitionSpec as P

gamma_less = 0.4
time_step = 0.1
vmem_bytes = 56 * 1024 * 1024


def divisor_up_to(number, limit):
    return max(d for d in range(1, limit + 1) if number % d == 0)


def hop(index, step, size, sign):
    if size & (size - 1) == 0:
        return index ^ step
    return (index + sign * step) % size


def fluxes(fields, direction):
    density, momentum, energy = fields[0], fields[1:4], fields[4]
    inverse = 1.0 / density
    velocity = momentum[direction] * inverse
    square = momentum[0] * momentum[0] + momentum[1] * momentum[1] + momentum[2] * momentum[2]
    pressure = gamma_less * (energy - 0.5 * square * inverse)
    out = [momentum[direction]]
    for column in range(3):
        product = momentum[column] * velocity
        if column == direction:
            product = product + pressure
        out.append(product)
    out.append((energy + pressure) * velocity)
    return out


def halves(value):
    high = value.astype(jnp.bfloat16)
    low = (value - high.astype(jnp.float32)).astype(jnp.bfloat16)
    return high, low


def split_outside(value):
    high = lax.reduce_precision(value, exponent_bits=8, mantissa_bits=7)
    return high.astype(jnp.bfloat16), (value - high).astype(jnp.bfloat16)


def dot(a, b):
    return jnp.dot(a, b, preferred_element_type=jnp.float32)


def call(body, name, order, operands, grid, in_specs, out_specs, out_shape, scratch=(), aliases=None, flops=0):
    scalars = tuple(order)
    moved = sum(4 * o.size for o in operands) + sum(4 * o.size for o in jax.tree.leaves(out_shape))
    return pl.pallas_call(
        body,
        name=name,
        grid_spec=pltpu.PrefetchScalarGridSpec(
            num_scalar_prefetch=len(scalars),
            grid=grid,
            in_specs=in_specs,
            out_specs=out_specs,
            scratch_shapes=list(scratch),
        ),
        out_shape=out_shape,
        input_output_aliases={} if aliases is None else aliases,
        compiler_params=pltpu.CompilerParams(vmem_limit_bytes=vmem_bytes),
        cost_estimate=pl.CostEstimate(flops=flops, bytes_accessed=moved, transcendentals=0),
    )(*scalars, *operands)


def pack_span_kernel(order, density, momentum, energy, piece):
    piece[0] = density[0]
    for column in range(3):
        piece[1 + column] = momentum[column, 0]
    piece[4] = energy[0]


def pack_span(order, chunk, chunks, density, momentum, energy):
    _, share, zl, nx = density.shape
    rows = share // chunks
    r = divisor_up_to(rows, 8)
    first = chunk * (rows // r)
    flat = pl.BlockSpec((1, r, zl, nx), lambda i, s: (s[0], first + i, 0, 0))
    return call(
        pack_span_kernel,
        f"pack_span_{chunk}",
        (order,),
        (density, momentum, energy),
        (rows // r,),
        [flat, pl.BlockSpec((3, 1, r, zl, nx), lambda i, s: (0, s[0], first + i, 0, 0)), flat],
        pl.BlockSpec((5, r, zl, nx), lambda i, s: (0, i, 0, 0)),
        jax.ShapeDtypeStruct((5, rows, zl, nx), jnp.float32),
    )


def span_kernel(n, weights, both, *refs):
    pieces, outs = refs[:n], refs[n:]
    _, r, zl, nx = pieces[0].shape
    nz = n * zl

    @pl.loop(0, r)
    def _(row):
        weight = weights[pl.program_id(0) * r + row]
        fields = [jnp.concatenate([p[f, row] for p in pieces], axis=0) for f in range(5)]
        for f, flux in enumerate(fluxes(fields, 2)):
            high, low = halves(jnp.concatenate([flux, weight * fields[f]], axis=0))
            total = dot(both[...], high)
            total = total[:nz] + total[nz:] + dot(both[:nz], low)
            for k, out in enumerate(outs):
                out[f, row] = total[k * zl : (k + 1) * zl]


def span_terms(chunk, weights, both, pieces):
    n = len(pieces)
    _, rows, zl, nx = pieces[0].shape
    r = divisor_up_to(rows, 2)
    nz = n * zl
    spec = pl.BlockSpec((5, r, zl, nx), lambda i, s: (0, i, 0, 0))
    return call(
        functools.partial(span_kernel, n),
        f"span_terms_{chunk}",
        (weights,),
        (both, *pieces),
        (rows // r,),
        [pl.BlockSpec(both.shape, lambda i, s: (0, 0))] + [spec] * n,
        [spec] * n,
        [jax.ShapeDtypeStruct(p.shape, jnp.float32) for p in pieces],
        flops=5 * rows * 6 * nz * 2 * nz * nx,
    )


def pack_wall_kernel(zl, density, momentum, energy, pieces, narrow):
    m, _, zz, rows, nx = pieces.shape
    lane = narrow.shape[-1]
    for half in range(nx // lane):
        lanes = slice(half * lane, (half + 1) * lane)
        narrow[half, 0] = density[:, lanes]
        for column in range(3):
            narrow[half, 1 + column] = momentum[column, :, lanes]
        narrow[half, 4] = energy[:, lanes]
    for z in range(zl):
        lines = pl.ds(z, rows, stride=zl)
        for half in range(nx // lane):
            lanes = slice(half * lane, (half + 1) * lane)
            for f in range(5):
                pieces[z // zz, f, z % zz, :, lanes] = narrow[half, f, lines, :]


def pack_wall(m, density, momentum, energy):
    jl, zl, nx = density.shape
    zz = zl // m
    lane = divisor_up_to(nx, 128)
    rows = divisor_up_to(jl, 32)
    flat = pl.BlockSpec((rows * zl, nx), lambda i: (i, 0))
    return call(
        functools.partial(pack_wall_kernel, zl),
        "pack_wall",
        (),
        (density.reshape(jl * zl, nx), momentum.reshape(3, jl * zl, nx), energy.reshape(jl * zl, nx)),
        (jl // rows,),
        [flat, pl.BlockSpec((3, rows * zl, nx), lambda i: (0, i, 0)), flat],
        pl.BlockSpec((m, 5, zz, rows, nx), lambda i: (0, 0, 0, i, 0)),
        jax.ShapeDtypeStruct((m, 5, zz, jl, nx), jnp.float32),
        scratch=[pltpu.VMEM((nx // lane, 5, rows * zl, lane), jnp.float32)],
    )


def wall_kernel(high, low, damping, pieces, outs, kept, flux_high, flux_low):
    m, _, _, jl, nx = pieces.shape
    ny = m * jl
    step = divisor_up_to(jl, 32)
    for f in range(5):
        kept[f, 0:8] = jnp.zeros((8, nx), jnp.float32)
        kept[f, 8 + ny : 16 + ny] = jnp.zeros((8, nx), jnp.float32)
    for k in range(m):

        @pl.loop(0, jl // step)
        def _(i):
            here = pl.ds(pl.multiple_of(i * step, step), step)
            there = pl.multiple_of(k * jl + i * step, step)
            fields = [pieces[k, f, 0, here, :] for f in range(5)]
            for f, flux in enumerate(fluxes(fields, 1)):
                kept[f, pl.ds(there + 8, step), :] = fields[f]
                flux_high[f, pl.ds(there, step), :], flux_low[f, pl.ds(there, step), :] = halves(flux)

    for k in range(m):
        first = k * jl
        rows = pl.ds(first, jl)

        @pl.loop(0, 5)
        def _(f):
            total = dot(high[rows, :], flux_high[f]) + dot(low[rows, :], flux_high[f])
            outs[k, f, 0] = total + dot(high[rows, :], flux_low[f])
            part = divisor_up_to(jl, 64)

            @pl.loop(0, jl // part)
            def _(i):
                at = pl.multiple_of(i * part, part)
                c = kept[f, pl.ds(first + at, part + 16), :]

                def shifted(offset):
                    return c[8 + offset : 8 + offset + part]

                fourth = (
                    shifted(-2) - 4.0 * shifted(-1) + 6.0 * shifted(0) - 4.0 * shifted(1) + shifted(2)
                )
                weight = damping[pl.ds(first + at, part), :]
                outs[k, f, 0, pl.ds(at, part), :] += weight * fourth


def wall_terms(operator, damping, pieces):
    m, _, zz, jl, nx = pieces.shape
    ny = m * jl
    high, low = split_outside(operator)
    spec = pl.BlockSpec((m, 5, 1, jl, nx), lambda i: (0, 0, i, 0, 0))
    whole = pl.BlockSpec((ny, ny), lambda i: (0, 0))
    return call(
        wall_kernel,
        "wall_terms",
        (),
        (high, low, damping.reshape(ny, 1), pieces),
        (zz,),
        [whole, whole, pl.BlockSpec((ny, 1), lambda i: (0, 0)), spec],
        spec,
        jax.ShapeDtypeStruct(pieces.shape, jnp.float32),
        scratch=[
            pltpu.VMEM((5, ny + 16, nx), jnp.float32),
            pltpu.VMEM((5, ny, nx), jnp.bfloat16),
            pltpu.VMEM((5, ny, nx), jnp.bfloat16),
        ],
        flops=6 * 5 * zz * ny * ny * nx,
    )


def base_kernel(zl, density, momentum, energy, pieces, *refs):
    outs, wall = refs[:3], refs[3]
    _, _, zz, rows, nx = pieces.shape
    lane = wall.shape[-1]
    for z in range(zl):
        lines = pl.ds(z, rows, stride=zl)
        for half in range(nx // lane):
            lanes = slice(half * lane, (half + 1) * lane)
            for f in range(5):
                wall[half, f, lines, :] = pieces[z // zz, f, z % zz, :, lanes]
    part = 16

    @pl.loop(0, rows * zl // part)
    def _(i):
        here = pl.ds(pl.multiple_of(i * part, part), part)
        fields = [density[here, :]] + [momentum[column, here, :] for column in range(3)] + [energy[here, :]]
        column = lax.broadcasted_iota(jnp.int32, (part, nx), 1)
        for f, flux in enumerate(fluxes(fields, 0)):
            first, last = flux[:, :1], flux[:, nx - 1 :]
            above1 = jnp.where(column >= nx - 1, last, pltpu.roll(flux, nx - 1, 1))
            above2 = jnp.where(column >= nx - 2, last, pltpu.roll(flux, nx - 2, 1))
            below1 = jnp.where(column < 1, first, pltpu.roll(flux, 1, 1))
            below2 = jnp.where(column < 2, first, pltpu.roll(flux, 2, 1))
            along = (8.0 * (above1 - below1) - (above2 - below2)) * (1.0 / 12.0)
            across = jnp.concatenate([wall[half, f, here, :] for half in range(wall.shape[0])], axis=1)
            value = fields[f] - time_step * (along + across)
            if f == 0:
                outs[0][here, :] = value
            elif f == 4:
                outs[2][here, :] = value
            else:
                outs[1][f - 1, here, :] = value


def base_fields(density, momentum, energy, pieces):
    m = pieces.shape[0]
    jl, zl, nx = density.shape
    zz = zl // m
    lane = divisor_up_to(nx, 128)
    rows = divisor_up_to(jl, 16)
    flat = pl.BlockSpec((rows * zl, nx), lambda i: (i, 0))
    three = pl.BlockSpec((3, rows * zl, nx), lambda i: (0, i, 0))
    shape = jax.ShapeDtypeStruct((jl * zl, nx), jnp.float32)
    outs = call(
        functools.partial(base_kernel, zl),
        "base_fields",
        (),
        (density.reshape(jl * zl, nx), momentum.reshape(3, jl * zl, nx), energy.reshape(jl * zl, nx), pieces),
        (jl // rows,),
        [flat, three, flat, pl.BlockSpec((m, 5, zz, rows, nx), lambda i: (0, 0, 0, i, 0))],
        [flat, three, flat],
        [shape, jax.ShapeDtypeStruct((3, jl * zl, nx), jnp.float32), shape],
        scratch=[pltpu.VMEM((nx // lane, 5, rows * zl, lane), jnp.float32)],
    )
    return outs


def add_span_kernel(order, density, momentum, energy, *refs):
    pieces, outs = refs[:-3], refs[-3:]
    for k, piece in enumerate(pieces):

        @pl.when(pl.program_id(0) == k)
        def _():
            outs[0][0] = density[0] - time_step * piece[0]
            for column in range(3):
                outs[1][column, 0] = momentum[column, 0] - time_step * piece[1 + column]
            outs[2][0] = energy[0] - time_step * piece[4]


def add_span(order, chunk, chunks, fields, pieces):
    share, zl, nx = fields[0].shape[1:]
    rows = share // chunks
    r = divisor_up_to(rows, 8)
    steps = rows // r
    first = chunk * steps
    flat = pl.BlockSpec((1, r, zl, nx), lambda p, i, s: (s[p], first + i, 0, 0))
    three = pl.BlockSpec((3, 1, r, zl, nx), lambda p, i, s: (0, s[p], first + i, 0, 0))

    def own(k):
        def index(p, i, s):
            return 0, jnp.where(p == k, i, jnp.where(p < k, 0, steps - 1)), 0, 0

        return pl.BlockSpec((5, r, zl, nx), index)

    return call(
        add_span_kernel,
        f"add_span_{chunk}",
        (order,),
        (*fields, *pieces),
        (len(pieces), steps),
        [flat, three, flat] + [own(k) for k in range(len(pieces))],
        [flat, three, flat],
        [jax.ShapeDtypeStruct(f.shape, f.dtype) for f in fields],
        aliases={1: 0, 2: 1, 3: 2},
    )


def after(value, earlier):
    if len(earlier) == 0:
        return value
    return lax.optimization_barrier((value, *earlier))[0]


class Sender:
    def __init__(self, axis, size, width):
        self.axis, self.size, self.width, self.far = axis, size, width, []

    def permute(self, piece, step, sign, earlier):
        pairs = [(i, hop(i, step, self.size, sign)) for i in range(self.size)]
        return lax.ppermute(after(piece, earlier), self.axis, pairs)

    def exchange(self, pieces, sign, earlier=()):
        pieces = list(pieces)
        first = self.size // 2
        sent = []
        for k in range(self.size - 1, first - 1, -1):
            held = [self.far[-self.width]] if len(self.far) >= self.width else []
            pieces[k] = self.permute(pieces[k], k, sign, [*held, *earlier])
            self.far.append(pieces[k])
            sent.append(pieces[k])
        for j, k in enumerate(range(1, first)):
            pieces[k] = self.permute(pieces[k], k, sign, [sent[j]])
        return pieces


def local(density, momentum, energy, wall_operator, span_operator, damping, *, chunks):
    jl, zl, nx = density.shape
    nz = span_operator.shape[0]
    m, n = lax.axis_size("gy"), lax.axis_size("gz")
    gy, gz = lax.axis_index("gy"), lax.axis_index("gz")
    share = jl // n
    chunks = divisor_up_to(share, chunks)
    rows = share // chunks

    span_to = [jnp.asarray(hop(gz, k, n, 1), jnp.int32).reshape(1) for k in range(n)]
    span_from = jnp.concatenate([jnp.asarray(hop(gz, k, n, -1), jnp.int32).reshape(1) for k in range(n)])
    by_share = (
        density.reshape(n, share, zl, nx),
        momentum.reshape(3, n, share, zl, nx),
        energy.reshape(n, share, zl, nx),
    )
    far, near = list(range(n // 2, n))[::-1], list(range(1, n // 2))
    sender = Sender("gz", n, 4)

    packs = [[pack_span(span_to[k], c, chunks, *by_share) for k in range(n)] for c in range(chunks)]
    packed = pack_wall(m, after(density, packs[0]), momentum, energy)
    wall_out = lax.all_to_all(packed, "gy", split_axis=0, concat_axis=0, tiled=True)
    span_out = [sender.exchange(packs[c], 1, [] if c == 0 else [packed]) for c in range(chunks)]

    identity = jnp.eye(nz, dtype=jnp.float32)
    fourth = 6.0 * identity
    for offset, factor in ((1, -4.0), (-1, -4.0), (2, 1.0), (-2, 1.0)):
        fourth = fourth + factor * jnp.roll(identity, offset, 1)

    def in_order_of_arrival(matrix):
        blocks = matrix.reshape(n, zl, n, zl)
        blocks = jnp.take(jnp.take(blocks, span_from, axis=0), span_from, axis=2)
        return blocks.reshape(nz, nz)

    both = jnp.concatenate([in_order_of_arrival(span_operator), in_order_of_arrival(fourth)], axis=1)
    both = jnp.concatenate(split_outside(both), axis=0)

    def weights(c):
        return lax.dynamic_slice_in_dim(damping, gy * jl + gz * share + c * rows, rows)

    span_back = [sender.exchange(span_terms(0, weights(0), both, span_out[0]), -1)]
    begun = span_out[-1][far[0]] if chunks > 1 else wall_out
    wall_back = wall_terms(wall_operator, damping, after(wall_out, [begun]))
    wall_back = lax.all_to_all(wall_back, "gy", split_axis=0, concat_axis=0, tiled=True)
    for c in range(1, chunks):
        span_back.append(sender.exchange(span_terms(c, weights(c), both, span_out[c]), -1))

    middle = span_back[0][far[n // 4]]
    fields = base_fields(density, momentum, energy, after(wall_back, [middle]))
    fields = (
        fields[0].reshape(n, share, zl, nx),
        fields[1].reshape(3, n, share, zl, nx),
        fields[2].reshape(n, share, zl, nx),
    )
    groups = [(c, [0, *near, *far]) for c in range(chunks - 1)]
    groups += [(chunks - 1, g) for g in ([0, *near], far[: n // 4], far[n // 4 :]) if g]
    for c, group in groups:
        order = jnp.concatenate([span_to[k] for k in group])
        fields = add_span(order, c, chunks, fields, [span_back[c][k] for k in group])
    return (
        fields[0].reshape(jl, zl, nx),
        fields[1].reshape(3, jl, zl, nx),
        fields[2].reshape(jl, zl, nx),
    )


def solution(mesh):
    in_specs = (P("gy", "gz", None), P(None, "gy", "gz", None), P("gy", "gz", None), P(), P(), P())
    out_specs = (P("gy", "gz", None), P(None, "gy", "gz", None), P("gy", "gz", None))
    return jax.shard_map(
        functools.partial(local, chunks=2), mesh=mesh, in_specs=in_specs, out_specs=out_specs, check_vma=False
    )
```

```python
import functools

import jax
import jax.numpy as jnp
from jax import lax
from jax.experimental import pallas as pl
from jax.experimental.pallas import tpu as pltpu
from jax.sharding import PartitionSpec as P

gamma_less = 0.4
time_step = 0.1
vmem_bytes = 63 * 1024 * 1024
WIDTH = 4


def divisor_up_to(number, limit):
    return max(d for d in range(1, limit + 1) if number % d == 0)


def hop(index, step, size, sign):
    if size & (size - 1) == 0:
        return index ^ step
    return (index + sign * step) % size


def fluxes(fields, direction):
    density, momentum, energy = fields[0], fields[1:4], fields[4]
    inverse = 1.0 / density
    velocity = momentum[direction] * inverse
    square = momentum[0] * momentum[0] + momentum[1] * momentum[1] + momentum[2] * momentum[2]
    pressure = gamma_less * (energy - 0.5 * square * inverse)
    out = [momentum[direction]]
    for column in range(3):
        product = momentum[column] * velocity
        if column == direction:
            product = product + pressure
        out.append(product)
    out.append((energy + pressure) * velocity)
    return out


def halves(value):
    high = value.astype(jnp.bfloat16)
    low = (value - high.astype(jnp.float32)).astype(jnp.bfloat16)
    return high, low


def split_outside(value):
    high = lax.reduce_precision(value, exponent_bits=8, mantissa_bits=7)
    return high.astype(jnp.bfloat16), (value - high).astype(jnp.bfloat16)


def dot(a, b):
    return jnp.dot(a, b, preferred_element_type=jnp.float32)


def call(body, name, order, operands, grid, in_specs, out_specs, out_shape, scratch=(), aliases=None, flops=0, mark=False, wait=()):
    scalars = tuple(order)
    moved = sum(4 * o.size for o in operands) + sum(4 * o.size for o in jax.tree.leaves(out_shape))
    if wait:
        begin = len(scalars) + len(operands)
        plain = body

        def body(*refs):
            plain(*refs[:begin], *refs[begin + len(wait) :])

        operands = [*operands, *wait]
        in_specs = [*in_specs, *[pl.BlockSpec(memory_space=pl.ANY)] * len(wait)]
    inner = body
    if mark:
        place = len(scalars) + len(operands) + len(out_shape)

        def body(*refs):
            inner(*refs[:place], *refs[place + 1 :])
            refs[place][...] = jnp.zeros_like(refs[place])

        out_specs = [*out_specs, pl.BlockSpec((8, 128), lambda *_: (0, 0))]
        out_shape = [*out_shape, jax.ShapeDtypeStruct((8, 128), jnp.float32)]
    return pl.pallas_call(
        body,
        name=name,
        grid_spec=pltpu.PrefetchScalarGridSpec(
            num_scalar_prefetch=len(scalars),
            grid=grid,
            in_specs=in_specs,
            out_specs=out_specs,
            scratch_shapes=list(scratch),
        ),
        out_shape=out_shape,
        input_output_aliases={} if aliases is None else aliases,
        compiler_params=pltpu.CompilerParams(vmem_limit_bytes=vmem_bytes),
        cost_estimate=pl.CostEstimate(flops=flops, bytes_accessed=moved, transcendentals=0),
    )(*scalars, *operands)


def pack_span_kernel(order, density, momentum, energy, piece):
    piece[0] = density[0]
    for column in range(3):
        piece[1 + column] = momentum[column, 0]
    piece[4] = energy[0]


def pack_span(order, chunk, chunks, density, momentum, energy, wait=()):
    _, share, zl, nx = density.shape
    rows = share // chunks
    r = divisor_up_to(rows, 8)
    first = chunk * (rows // r)
    flat = pl.BlockSpec((1, r, zl, nx), lambda i, s: (s[0], first + i, 0, 0))
    return call(
        pack_span_kernel,
        f"pack_span_{chunk}",
        (order,),
        (density, momentum, energy),
        (rows // r,),
        [flat, pl.BlockSpec((3, 1, r, zl, nx), lambda i, s: (0, s[0], first + i, 0, 0)), flat],
        pl.BlockSpec((5, r, zl, nx), lambda i, s: (0, i, 0, 0)),
        jax.ShapeDtypeStruct((5, rows, zl, nx), jnp.float32),
        wait=wait,
    )


def span_kernel(n, weights, both, *refs):
    pieces, outs = refs[:n], refs[n:]
    _, r, zl, nx = pieces[0].shape
    nz = n * zl

    @pl.loop(0, r)
    def _(row):
        weight = weights[pl.program_id(0) * r + row]
        fields = [jnp.concatenate([p[f, row] for p in pieces], axis=0) for f in range(5)]
        for f, flux in enumerate(fluxes(fields, 2)):
            high, low = halves(jnp.concatenate([flux, weight * fields[f]], axis=0))
            total = dot(both[...], high)
            total = total[:nz] + total[nz:] + dot(both[:nz], low)
            for k, out in enumerate(outs):
                out[f, row] = total[k * zl : (k + 1) * zl]


def span_terms(chunk, weights, both, pieces):
    n = len(pieces)
    _, rows, zl, nx = pieces[0].shape
    r = divisor_up_to(rows, 2)
    nz = n * zl
    spec = pl.BlockSpec((5, r, zl, nx), lambda i, s: (0, i, 0, 0))
    return call(
        functools.partial(span_kernel, n),
        f"span_terms_{chunk}",
        (weights,),
        (both, *pieces),
        (rows // r,),
        [pl.BlockSpec(both.shape, lambda i, s: (0, 0))] + [spec] * n,
        [spec] * n,
        [jax.ShapeDtypeStruct(p.shape, jnp.float32) for p in pieces],
        flops=5 * rows * 6 * nz * 2 * nz * nx,
    )


def pack_wall_kernel(zl, density, momentum, energy, pieces, narrow):
    m, _, zz, rows, nx = pieces.shape
    lane = narrow.shape[-1]
    for half in range(nx // lane):
        lanes = slice(half * lane, (half + 1) * lane)
        narrow[half, 0] = density[:, lanes]
        for column in range(3):
            narrow[half, 1 + column] = momentum[column, :, lanes]
        narrow[half, 4] = energy[:, lanes]
    for z in range(zl):
        lines = pl.ds(z, rows, stride=zl)
        for half in range(nx // lane):
            lanes = slice(half * lane, (half + 1) * lane)
            for f in range(5):
                pieces[z // zz, f, z % zz, :, lanes] = narrow[half, f, lines, :]


def pack_wall(m, density, momentum, energy, wait=()):
    jl, zl, nx = density.shape
    zz = zl // m
    lane = divisor_up_to(nx, 128)
    rows = divisor_up_to(jl, 32)
    flat = pl.BlockSpec((rows * zl, nx), lambda i: (i, 0))
    return call(
        functools.partial(pack_wall_kernel, zl),
        "pack_wall",
        (),
        (density.reshape(jl * zl, nx), momentum.reshape(3, jl * zl, nx), energy.reshape(jl * zl, nx)),
        (jl // rows,),
        [flat, pl.BlockSpec((3, rows * zl, nx), lambda i: (0, i, 0)), flat],
        pl.BlockSpec((m, 5, zz, rows, nx), lambda i: (0, 0, 0, i, 0)),
        jax.ShapeDtypeStruct((m, 5, zz, jl, nx), jnp.float32),
        wait=wait,
        scratch=[pltpu.VMEM((nx // lane, 5, rows * zl, lane), jnp.float32)],
    )


def wall_kernel(both, damping, pieces, *refs):
    outs, kept, flux_high, flux_low = refs[-4:]
    m, _, _, jl, nx = pieces.shape
    ny = m * jl
    step = divisor_up_to(jl, 64)
    for f in range(5):
        kept[f, 0:8] = jnp.zeros((8, nx), jnp.float32)
        kept[f, 8 + ny : 16 + ny] = jnp.zeros((8, nx), jnp.float32)
    for k in range(m):

        @pl.loop(0, jl // step)
        def _(i):
            here = pl.ds(pl.multiple_of(i * step, step), step)
            there = pl.multiple_of(k * jl + i * step, step)
            fields = [pieces[k, f, 0, here, :] for f in range(5)]
            for f, flux in enumerate(fluxes(fields, 1)):
                kept[f, pl.ds(there + 8, step), :] = fields[f]
                flux_high[f, pl.ds(there, step), :], flux_low[f, pl.ds(there, step), :] = halves(flux)

    @pl.loop(0, 5)
    def _(f):
        large = dot(both[...], flux_high[f])
        total = large[:ny] + large[ny:] + dot(both[:ny], flux_low[f])
        for k in range(m):
            outs[k, f, 0] = total[k * jl : (k + 1) * jl]
        part = divisor_up_to(jl, 128)
        for k in range(m):

            @pl.loop(0, jl // part)
            def _(i):
                at = pl.multiple_of(i * part, part)
                c = kept[f, pl.ds(k * jl + at, part + 16), :]

                def shifted(offset):
                    return c[8 + offset : 8 + offset + part]

                fourth = (
                    shifted(-2) - 4.0 * shifted(-1) + 6.0 * shifted(0) - 4.0 * shifted(1) + shifted(2)
                )
                weight = damping[pl.ds(k * jl + at, part), :]
                outs[k, f, 0, pl.ds(at, part), :] += weight * fourth


def wall_terms(both, damping, pieces, part, parts, made=(), wait=()):
    m, _, zz, jl, nx = pieces.shape
    ny = m * jl
    steps = zz // parts
    spec = pl.BlockSpec((m, 5, 1, jl, nx), lambda i: (0, 0, part * steps + i, 0, 0))
    return call(
        wall_kernel,
        f"wall_terms_{part}",
        (),
        (both, damping, pieces, *made),
        (steps,),
        [pl.BlockSpec((2 * ny, ny), lambda i: (0, 0)), pl.BlockSpec((ny, 1), lambda i: (0, 0)), spec]
        + [pl.BlockSpec(memory_space=pl.ANY)] * len(made),
        [spec],
        [jax.ShapeDtypeStruct(pieces.shape, jnp.float32)],
        scratch=[
            pltpu.VMEM((5, ny + 16, nx), jnp.float32),
            pltpu.VMEM((5, ny, nx), jnp.bfloat16),
            pltpu.VMEM((5, ny, nx), jnp.bfloat16),
        ],
        aliases={3: 0} if made else None,
        wait=wait,
        flops=6 * 5 * steps * ny * ny * nx,
    )


def base_kernel(zl, density, momentum, energy, pieces, *refs):
    outs, wall = refs[:3], refs[3]
    _, _, zz, rows, nx = pieces.shape
    lane = wall.shape[-1]
    for z in range(zl):
        lines = pl.ds(z, rows, stride=zl)
        for half in range(nx // lane):
            lanes = slice(half * lane, (half + 1) * lane)
            for f in range(5):
                wall[half, f, lines, :] = pieces[z // zz, f, z % zz, :, lanes]
    part = divisor_up_to(rows * zl, 64)

    @pl.loop(0, rows * zl // part)
    def _(i):
        here = pl.ds(pl.multiple_of(i * part, part), part)
        fields = [density[here, :]] + [momentum[column, here, :] for column in range(3)] + [energy[here, :]]
        column = lax.broadcasted_iota(jnp.int32, (part, nx), 1)
        for f, flux in enumerate(fluxes(fields, 0)):
            first, last = flux[:, :1], flux[:, nx - 1 :]
            above1 = jnp.where(column >= nx - 1, last, pltpu.roll(flux, nx - 1, 1))
            above2 = jnp.where(column >= nx - 2, last, pltpu.roll(flux, nx - 2, 1))
            below1 = jnp.where(column < 1, first, pltpu.roll(flux, 1, 1))
            below2 = jnp.where(column < 2, first, pltpu.roll(flux, 2, 1))
            along = (8.0 * (above1 - below1) - (above2 - below2)) * (1.0 / 12.0)
            across = jnp.concatenate([wall[half, f, here, :] for half in range(wall.shape[0])], axis=1)
            value = fields[f] - time_step * (along + across)
            if f == 0:
                outs[0][here, :] = value
            elif f == 4:
                outs[2][here, :] = value
            else:
                outs[1][f - 1, here, :] = value


def base_fields(density, momentum, energy, pieces, wait=()):
    m = pieces.shape[0]
    jl, zl, nx = density.shape
    zz = zl // m
    lane = divisor_up_to(nx, 128)
    rows = divisor_up_to(jl, 16)
    flat = pl.BlockSpec((rows * zl, nx), lambda i: (i, 0))
    three = pl.BlockSpec((3, rows * zl, nx), lambda i: (0, i, 0))
    shape = jax.ShapeDtypeStruct((jl * zl, nx), jnp.float32)
    outs = call(
        functools.partial(base_kernel, zl),
        "base_fields",
        (),
        (density.reshape(jl * zl, nx), momentum.reshape(3, jl * zl, nx), energy.reshape(jl * zl, nx), pieces),
        (jl // rows,),
        [flat, three, flat, pl.BlockSpec((m, 5, zz, rows, nx), lambda i: (0, 0, 0, i, 0))],
        [flat, three, flat],
        [shape, jax.ShapeDtypeStruct((3, jl * zl, nx), jnp.float32), shape],
        scratch=[pltpu.VMEM((nx // lane, 5, rows * zl, lane), jnp.float32)],
        mark=True,
        wait=wait,
    )
    return outs


def add_span_kernel(order, density, momentum, energy, *refs):
    pieces, outs = refs[:-3], refs[-3:]
    for k, piece in enumerate(pieces):

        @pl.when(pl.program_id(0) == k)
        def _():
            outs[0][0] = density[0] - time_step * piece[0]
            for column in range(3):
                outs[1][column, 0] = momentum[column, 0] - time_step * piece[1 + column]
            outs[2][0] = energy[0] - time_step * piece[4]


def add_span(order, chunk, chunks, fields, pieces, wait=()):
    share, zl, nx = fields[0].shape[1:]
    rows = share // chunks
    r = divisor_up_to(rows, 8)
    steps = rows // r
    first = chunk * steps
    flat = pl.BlockSpec((1, r, zl, nx), lambda p, i, s: (s[p], first + i, 0, 0))
    three = pl.BlockSpec((3, 1, r, zl, nx), lambda p, i, s: (0, s[p], first + i, 0, 0))

    def own(k):
        def index(p, i, s):
            return 0, jnp.where(p == k, i, jnp.where(p < k, 0, steps - 1)), 0, 0

        return pl.BlockSpec((5, r, zl, nx), index)

    return call(
        add_span_kernel,
        f"add_span_{chunk}",
        (order,),
        (*fields, *pieces),
        (len(pieces), steps),
        [flat, three, flat] + [own(k) for k in range(len(pieces))],
        [flat, three, flat],
        [jax.ShapeDtypeStruct(f.shape, f.dtype) for f in fields],
        aliases={1: 0, 2: 1, 3: 2},
        mark=True,
        wait=wait,
    )


def after(value, wait):
    if not wait:
        return value
    anywhere = pl.BlockSpec(memory_space=pl.ANY)
    return pl.pallas_call(
        lambda *refs: None,
        name="after",
        in_specs=[anywhere] * (1 + len(wait)),
        out_specs=anywhere,
        out_shape=jax.ShapeDtypeStruct(value.shape, value.dtype),
        input_output_aliases={0: 0},
        compiler_params=pltpu.CompilerParams(vmem_limit_bytes=vmem_bytes),
        cost_estimate=pl.CostEstimate(flops=0, bytes_accessed=0, transcendentals=0),
    )(value, *wait)


class Sender:
    def __init__(self, axis, size, width):
        self.axis, self.size, self.width, self.far = axis, size, width, []

    def permute(self, piece, step, sign):
        pairs = [(i, hop(i, step, self.size, sign)) for i in range(self.size)]
        return lax.ppermute(piece, self.axis, pairs)

    def send_far(self, make, steps, sign, wait=()):
        out = {}
        for k in steps:
            held = [self.far[-self.width]] if len(self.far) >= self.width else []
            out[k] = self.permute(make(k, [*held, *wait]), k, sign)
            self.far.append(out[k])
        return out

    def send_near(self, make, steps, sign, begin):
        return {
            k: self.permute(make(k, self.far[: begin + j][-1:]), k, sign) for j, k in enumerate(steps)
        }


def local(density, momentum, energy, wall_operator, span_operator, damping, *, chunks):
    jl, zl, nx = density.shape
    ny, nz = wall_operator.shape[0], span_operator.shape[0]
    m, n = lax.axis_size("gy"), lax.axis_size("gz")
    gy, gz = lax.axis_index("gy"), lax.axis_index("gz")
    share = jl // n
    chunks = divisor_up_to(share, chunks)
    rows = share // chunks

    span_to = [jnp.asarray(hop(gz, k, n, 1), jnp.int32).reshape(1) for k in range(n)]
    span_from = jnp.concatenate([jnp.asarray(hop(gz, k, n, -1), jnp.int32).reshape(1) for k in range(n)])
    by_share = (
        density.reshape(n, share, zl, nx),
        momentum.reshape(3, n, share, zl, nx),
        energy.reshape(n, share, zl, nx),
    )
    far, near = list(range(n // 2, n))[::-1], list(range(1, n // 2))
    count = len(far)
    sender = Sender("gz", n, WIDTH)

    def pack(c):
        return lambda k, wait: pack_span(span_to[k], c, chunks, *by_share, wait=wait)

    def ordered(pieces):
        return [pieces[k] for k in range(n)]

    first_far = sender.send_far(pack(0), far, 1)
    first_near = sender.send_near(pack(0), near, 1, 0)
    span_out = [ordered({0: pack(0)(0, ()), **first_far, **first_near})]
    packed = pack_wall(m, density, momentum, energy, [first_near[k] for k in near[:1]])
    wall_out = lax.all_to_all(packed, "gy", split_axis=0, concat_axis=0, tiled=True)
    for c in range(1, chunks):
        later_far = sender.send_far(pack(c), far, 1, [packed])
        later_near = sender.send_near(pack(c), near, 1, c * count)
        span_out.append(ordered({0: pack(c)(0, ()), **later_far, **later_near}))

    identity = jnp.eye(nz, dtype=jnp.float32)
    fourth = 6.0 * identity
    for offset, factor in ((1, -4.0), (-1, -4.0), (2, 1.0), (-2, 1.0)):
        fourth = fourth + factor * jnp.roll(identity, offset, 1)

    def in_order_of_arrival(matrix):
        blocks = matrix.reshape(n, zl, n, zl)
        blocks = jnp.take(jnp.take(blocks, span_from, axis=0), span_from, axis=2)
        return blocks.reshape(nz, nz)

    both = jnp.concatenate([in_order_of_arrival(span_operator), in_order_of_arrival(fourth)], axis=1)
    both = jnp.concatenate(split_outside(both), axis=0)
    wall_both = jnp.concatenate(split_outside(wall_operator), axis=0)

    def weights(c):
        return lax.dynamic_slice_in_dim(damping, gy * jl + gz * share + c * rows, rows)

    def back(c):
        pieces = span_terms(c, weights(c), both, span_out[c])
        return pieces, lambda k, wait: after(pieces[k], wait)

    zz = zl // m
    parts = divisor_up_to(zz, 2)
    wall_back = ()
    for part in range(parts):
        begun = sender.far[: count + 1] if part == 0 else sender.far[count + part : count + part + 1]
        wall_back = wall_terms(wall_both, damping.reshape(ny, 1), wall_out, part, parts, wall_back, begun)
    wall_back = lax.all_to_all(wall_back[0], "gy", split_axis=0, concat_axis=0, tiled=True)

    pieces, make = back(0)
    far_back = sender.send_far(make, far, -1)
    near_back = sender.send_near(make, near, -1, chunks * count)
    span_back = [ordered({0: pieces[0], **far_back, **near_back})]
    held = sender.far[-(1 + count // 4) :][:1]
    *fields, mark = base_fields(density, momentum, energy, wall_back, [*held, *near_back.values()])
    fields = (
        fields[0].reshape(n, share, zl, nx),
        fields[1].reshape(3, n, share, zl, nx),
        fields[2].reshape(n, share, zl, nx),
    )

    def add(c, group, wait=()):
        order = jnp.concatenate([span_to[k] for k in group])
        *out, mark = add_span(order, c, chunks, fields, [span_back[c][k] for k in group], wait)
        return out, mark

    for c in range(1, chunks):
        pieces, make = back(c)
        far_back = sender.send_far(make, far[:1], -1)
        far_back |= sender.send_far(make, far[1:2], -1, [mark])
        far_back |= sender.send_far(make, far[2:], -1)
        fields, mark = add(c - 1, [0, *near, *far], [far_back[far[0]]])
        begin = (chunks + c) * count + 2
        near_back = sender.send_near(make, near[:-1], -1, begin)
        near_back |= {k: sender.permute(make(k, [mark, far_back[far[-2]]]), k, -1) for k in near[-1:]}
        span_back.append(ordered({0: pieces[0], **far_back, **near_back}))
    last = chunks - 1
    groups = [(last, [0, *near]), (last, far[: count // 2]), (last, far[count // 2 :])]
    for c, group in groups:
        if group:
            fields, _ = add(c, group)
    return (
        fields[0].reshape(jl, zl, nx),
        fields[1].reshape(3, jl, zl, nx),
        fields[2].reshape(jl, zl, nx),
    )


def solution(mesh):
    in_specs = (P("gy", "gz", None), P(None, "gy", "gz", None), P("gy", "gz", None), P(), P(), P())
    out_specs = (P("gy", "gz", None), P(None, "gy", "gz", None), P("gy", "gz", None))
    return jax.shard_map(
        functools.partial(local, chunks=2), mesh=mesh, in_specs=in_specs, out_specs=out_specs, check_vma=False
    )
```

```python
import functools

import jax
import jax.numpy as jnp
from jax import lax
from jax.experimental import pallas as pl
from jax.experimental.pallas import tpu as pltpu
from jax.sharding import PartitionSpec as P

gamma_less = 0.4
time_step = 0.1
vmem_bytes = 63 * 1024 * 1024
WIDTH = 99
NEAR = 1


def divisor_up_to(number, limit):
    return max(d for d in range(1, limit + 1) if number % d == 0)


def hop(index, step, size, sign):
    if size & (size - 1) == 0:
        return index ^ step
    return (index + sign * step) % size


def fluxes(fields, direction):
    density, momentum, energy = fields[0], fields[1:4], fields[4]
    inverse = 1.0 / density
    velocity = momentum[direction] * inverse
    square = momentum[0] * momentum[0] + momentum[1] * momentum[1] + momentum[2] * momentum[2]
    pressure = gamma_less * (energy - 0.5 * square * inverse)
    out = [momentum[direction]]
    for column in range(3):
        product = momentum[column] * velocity
        if column == direction:
            product = product + pressure
        out.append(product)
    out.append((energy + pressure) * velocity)
    return out


def halves(value):
    high = value.astype(jnp.bfloat16)
    low = (value - high.astype(jnp.float32)).astype(jnp.bfloat16)
    return high, low


def split_outside(value):
    high = lax.reduce_precision(value, exponent_bits=8, mantissa_bits=7)
    return high.astype(jnp.bfloat16), (value - high).astype(jnp.bfloat16)


def dot(a, b):
    return jnp.dot(a, b, preferred_element_type=jnp.float32)


def call(body, name, order, operands, grid, in_specs, out_specs, out_shape, scratch=(), aliases=None, flops=0, mark=False, wait=()):
    scalars = tuple(order)
    moved = sum(4 * o.size for o in operands) + sum(4 * o.size for o in jax.tree.leaves(out_shape))
    if wait:
        begin = len(scalars) + len(operands)
        plain = body

        def body(*refs):
            plain(*refs[:begin], *refs[begin + len(wait) :])

        operands = [*operands, *wait]
        in_specs = [*in_specs, *[pl.BlockSpec(memory_space=pl.ANY)] * len(wait)]
    inner = body
    if mark:
        place = len(scalars) + len(operands) + len(out_shape)

        def body(*refs):
            inner(*refs[:place], *refs[place + 1 :])
            refs[place][...] = jnp.zeros_like(refs[place])

        out_specs = [*out_specs, pl.BlockSpec((8, 128), lambda *_: (0, 0))]
        out_shape = [*out_shape, jax.ShapeDtypeStruct((8, 128), jnp.float32)]
    return pl.pallas_call(
        body,
        name=name,
        grid_spec=pltpu.PrefetchScalarGridSpec(
            num_scalar_prefetch=len(scalars),
            grid=grid,
            in_specs=in_specs,
            out_specs=out_specs,
            scratch_shapes=list(scratch),
        ),
        out_shape=out_shape,
        input_output_aliases={} if aliases is None else aliases,
        compiler_params=pltpu.CompilerParams(vmem_limit_bytes=vmem_bytes),
        cost_estimate=pl.CostEstimate(flops=flops, bytes_accessed=moved, transcendentals=0),
    )(*scalars, *operands)


def pack_span_kernel(order, density, momentum, energy, piece):
    piece[0] = density[0]
    for column in range(3):
        piece[1 + column] = momentum[column, 0]
    piece[4] = energy[0]


def pack_span(order, chunk, chunks, density, momentum, energy, wait=()):
    _, share, zl, nx = density.shape
    rows = share // chunks
    r = divisor_up_to(rows, 8)
    first = chunk * (rows // r)
    flat = pl.BlockSpec((1, r, zl, nx), lambda i, s: (s[0], first + i, 0, 0))
    return call(
        pack_span_kernel,
        f"pack_span_{chunk}",
        (order,),
        (density, momentum, energy),
        (rows // r,),
        [flat, pl.BlockSpec((3, 1, r, zl, nx), lambda i, s: (0, s[0], first + i, 0, 0)), flat],
        pl.BlockSpec((5, r, zl, nx), lambda i, s: (0, i, 0, 0)),
        jax.ShapeDtypeStruct((5, rows, zl, nx), jnp.float32),
        wait=wait,
    )


def span_kernel(n, weights, both, *refs):
    pieces, outs = refs[:n], refs[n:]
    _, r, zl, nx = pieces[0].shape
    nz = n * zl

    @pl.loop(0, r)
    def _(row):
        weight = weights[pl.program_id(0) * r + row]
        fields = [jnp.concatenate([p[f, row] for p in pieces], axis=0) for f in range(5)]
        for f, flux in enumerate(fluxes(fields, 2)):
            high, low = halves(jnp.concatenate([flux, weight * fields[f]], axis=0))
            total = dot(both[...], high)
            total = total[:nz] + total[nz:] + dot(both[:nz], low)
            for k, out in enumerate(outs):
                out[f, row] = total[k * zl : (k + 1) * zl]


def span_terms(chunk, weights, both, pieces):
    n = len(pieces)
    _, rows, zl, nx = pieces[0].shape
    r = divisor_up_to(rows, 2)
    nz = n * zl
    spec = pl.BlockSpec((5, r, zl, nx), lambda i, s: (0, i, 0, 0))
    return call(
        functools.partial(span_kernel, n),
        f"span_terms_{chunk}",
        (weights,),
        (both, *pieces),
        (rows // r,),
        [pl.BlockSpec(both.shape, lambda i, s: (0, 0))] + [spec] * n,
        [spec] * n,
        [jax.ShapeDtypeStruct(p.shape, jnp.float32) for p in pieces],
        flops=5 * rows * 6 * nz * 2 * nz * nx,
    )


def pack_wall_kernel(zl, order, density, momentum, energy, *refs):
    pieces, narrow = refs[:-1], refs[-1]
    _, zz, rows, nx = pieces[0].shape
    lane = narrow.shape[-1]
    for half in range(nx // lane):
        lanes = slice(half * lane, (half + 1) * lane)
        narrow[half, 0] = density[:, lanes]
        for column in range(3):
            narrow[half, 1 + column] = momentum[column, :, lanes]
        narrow[half, 4] = energy[:, lanes]
    for k, piece in enumerate(pieces):
        for z in range(zz):
            lines = pl.ds(order[k] * zz + z, rows, stride=zl)
            for half in range(nx // lane):
                lanes = slice(half * lane, (half + 1) * lane)
                for f in range(5):
                    piece[f, z, :, lanes] = narrow[half, f, lines, :]


def pack_wall(blocks, density, momentum, energy, wait=()):
    m = blocks.shape[0]
    jl, zl, nx = density.shape
    zz = zl // m
    lane = divisor_up_to(nx, 128)
    rows = divisor_up_to(jl, 32)
    flat = pl.BlockSpec((rows * zl, nx), lambda i, s: (i, 0))
    return call(
        functools.partial(pack_wall_kernel, zl),
        "pack_wall",
        (blocks,),
        (density.reshape(jl * zl, nx), momentum.reshape(3, jl * zl, nx), energy.reshape(jl * zl, nx)),
        (jl // rows,),
        [flat, pl.BlockSpec((3, rows * zl, nx), lambda i, s: (0, i, 0)), flat],
        [pl.BlockSpec((5, zz, rows, nx), lambda i, s: (0, 0, i, 0))] * m,
        [jax.ShapeDtypeStruct((5, zz, jl, nx), jnp.float32)] * m,
        wait=wait,
        scratch=[pltpu.VMEM((nx // lane, 5, rows * zl, lane), jnp.float32)],
    )


def wall_kernel(m, order, both, damping, *refs):
    pieces, outs = refs[:m], refs[-4 - m : -4]
    kept, flux_high, flux_low, summed = refs[-4:]
    jl, nx = pieces[0].shape[2:]
    ny = m * jl
    step = divisor_up_to(jl, 64)
    for f in range(5):
        kept[f, 0:8] = jnp.zeros((8, nx), jnp.float32)
        kept[f, 8 + ny : 16 + ny] = jnp.zeros((8, nx), jnp.float32)
    for k in range(m):

        @pl.loop(0, jl // step)
        def _(i):
            here = pl.ds(pl.multiple_of(i * step, step), step)
            there = pl.multiple_of(order[k] * jl + i * step, step)
            fields = [pieces[k][f, 0, here, :] for f in range(5)]
            for f, flux in enumerate(fluxes(fields, 1)):
                kept[f, pl.ds(there + 8, step), :] = fields[f]
                flux_high[f, pl.ds(there, step), :], flux_low[f, pl.ds(there, step), :] = halves(flux)

    @pl.loop(0, 5)
    def _(f):
        large = dot(both[...], flux_high[f])
        summed[...] = large[:ny] + large[ny:] + dot(both[:ny], flux_low[f])
        part = divisor_up_to(jl, 128)
        for k in range(m):

            @pl.loop(0, jl // part)
            def _(i):
                at = pl.multiple_of(i * part, part)
                there = pl.multiple_of(order[k] * jl + at, part)
                c = kept[f, pl.ds(there, part + 16), :]

                def shifted(offset):
                    return c[8 + offset : 8 + offset + part]

                fourth = (
                    shifted(-2) - 4.0 * shifted(-1) + 6.0 * shifted(0) - 4.0 * shifted(1) + shifted(2)
                )
                rows = pl.ds(there, part)
                outs[k][f, 0, pl.ds(at, part), :] = summed[rows, :] + damping[rows, :] * fourth


def wall_terms(blocks, both, damping, pieces, part, parts, made=(), wait=()):
    m = len(pieces)
    _, zz, jl, nx = pieces[0].shape
    ny = m * jl
    steps = zz // parts
    spec = pl.BlockSpec((5, 1, jl, nx), lambda i, s: (0, part * steps + i, 0, 0))
    return call(
        functools.partial(wall_kernel, m),
        f"wall_terms_{part}",
        (blocks,),
        (both, damping, *pieces, *made),
        (steps,),
        [pl.BlockSpec((2 * ny, ny), lambda i, s: (0, 0)), pl.BlockSpec((ny, 1), lambda i, s: (0, 0))]
        + [spec] * m
        + [pl.BlockSpec(memory_space=pl.ANY)] * len(made),
        [spec] * m,
        [jax.ShapeDtypeStruct(p.shape, jnp.float32) for p in pieces],
        scratch=[
            pltpu.VMEM((5, ny + 16, nx), jnp.float32),
            pltpu.VMEM((5, ny, nx), jnp.bfloat16),
            pltpu.VMEM((5, ny, nx), jnp.bfloat16),
            pltpu.VMEM((ny, nx), jnp.float32),
        ],
        aliases={3 + m + k: k for k in range(m)} if made else None,
        wait=wait,
        flops=6 * 5 * steps * ny * ny * nx,
    )


def base_kernel(m, zl, order, density, momentum, energy, *refs):
    pieces, outs, wall = refs[:m], refs[m : m + 3], refs[m + 3]
    _, zz, rows, nx = pieces[0].shape
    lane = wall.shape[-1]
    for k, piece in enumerate(pieces):
        for z in range(zz):
            lines = pl.ds(order[k] * zz + z, rows, stride=zl)
            for half in range(nx // lane):
                lanes = slice(half * lane, (half + 1) * lane)
                for f in range(5):
                    wall[half, f, lines, :] = piece[f, z, :, lanes]
    part = divisor_up_to(rows * zl, 64)

    @pl.loop(0, rows * zl // part)
    def _(i):
        here = pl.ds(pl.multiple_of(i * part, part), part)
        fields = [density[here, :]] + [momentum[column, here, :] for column in range(3)] + [energy[here, :]]
        column = lax.broadcasted_iota(jnp.int32, (part, nx), 1)
        for f, flux in enumerate(fluxes(fields, 0)):
            first, last = flux[:, :1], flux[:, nx - 1 :]
            above1 = jnp.where(column >= nx - 1, last, pltpu.roll(flux, nx - 1, 1))
            above2 = jnp.where(column >= nx - 2, last, pltpu.roll(flux, nx - 2, 1))
            below1 = jnp.where(column < 1, first, pltpu.roll(flux, 1, 1))
            below2 = jnp.where(column < 2, first, pltpu.roll(flux, 2, 1))
            along = (8.0 * (above1 - below1) - (above2 - below2)) * (1.0 / 12.0)
            across = jnp.concatenate([wall[half, f, here, :] for half in range(wall.shape[0])], axis=1)
            value = fields[f] - time_step * (along + across)
            if f == 0:
                outs[0][here, :] = value
            elif f == 4:
                outs[2][here, :] = value
            else:
                outs[1][f - 1, here, :] = value


def base_fields(blocks, density, momentum, energy, pieces, wait=()):
    m = len(pieces)
    jl, zl, nx = density.shape
    zz = zl // m
    lane = divisor_up_to(nx, 128)
    rows = divisor_up_to(jl, 16)
    flat = pl.BlockSpec((rows * zl, nx), lambda i, s: (i, 0))
    three = pl.BlockSpec((3, rows * zl, nx), lambda i, s: (0, i, 0))
    shape = jax.ShapeDtypeStruct((jl * zl, nx), jnp.float32)
    outs = call(
        functools.partial(base_kernel, m, zl),
        "base_fields",
        (blocks,),
        (density.reshape(jl * zl, nx), momentum.reshape(3, jl * zl, nx), energy.reshape(jl * zl, nx), *pieces),
        (jl // rows,),
        [flat, three, flat] + [pl.BlockSpec((5, zz, rows, nx), lambda i, s: (0, 0, i, 0))] * m,
        [flat, three, flat],
        [shape, jax.ShapeDtypeStruct((3, jl * zl, nx), jnp.float32), shape],
        scratch=[pltpu.VMEM((nx // lane, 5, rows * zl, lane), jnp.float32)],
        mark=True,
        wait=wait,
    )
    return outs


def add_span_kernel(order, density, momentum, energy, *refs):
    pieces, outs = refs[:-3], refs[-3:]
    for k, piece in enumerate(pieces):

        @pl.when(pl.program_id(0) == k)
        def _():
            outs[0][0] = density[0] - time_step * piece[0]
            for column in range(3):
                outs[1][column, 0] = momentum[column, 0] - time_step * piece[1 + column]
            outs[2][0] = energy[0] - time_step * piece[4]


def add_span(order, chunk, chunks, fields, pieces, wait=()):
    share, zl, nx = fields[0].shape[1:]
    rows = share // chunks
    r = divisor_up_to(rows, 8)
    steps = rows // r
    first = chunk * steps
    flat = pl.BlockSpec((1, r, zl, nx), lambda p, i, s: (s[p], first + i, 0, 0))
    three = pl.BlockSpec((3, 1, r, zl, nx), lambda p, i, s: (0, s[p], first + i, 0, 0))

    def own(k):
        def index(p, i, s):
            return 0, jnp.where(p == k, i, jnp.where(p < k, 0, steps - 1)), 0, 0

        return pl.BlockSpec((5, r, zl, nx), index)

    return call(
        add_span_kernel,
        f"add_span_{chunk}",
        (order,),
        (*fields, *pieces),
        (len(pieces), steps),
        [flat, three, flat] + [own(k) for k in range(len(pieces))],
        [flat, three, flat],
        [jax.ShapeDtypeStruct(f.shape, f.dtype) for f in fields],
        aliases={1: 0, 2: 1, 3: 2},
        mark=True,
        wait=wait,
    )


def after(value, wait):
    if not wait:
        return value
    anywhere = pl.BlockSpec(memory_space=pl.ANY)
    return pl.pallas_call(
        lambda *refs: None,
        name="after",
        in_specs=[anywhere] * (1 + len(wait)),
        out_specs=anywhere,
        out_shape=jax.ShapeDtypeStruct(value.shape, value.dtype),
        input_output_aliases={0: 0},
        compiler_params=pltpu.CompilerParams(vmem_limit_bytes=vmem_bytes),
        cost_estimate=pl.CostEstimate(flops=0, bytes_accessed=0, transcendentals=0),
    )(value, *wait)


class Sender:
    def __init__(self, axis, size, width):
        self.axis, self.size, self.width, self.far = axis, size, width, []

    def permute(self, piece, step, sign):
        pairs = [(i, hop(i, step, self.size, sign)) for i in range(self.size)]
        return lax.ppermute(piece, self.axis, pairs)

    def send_far(self, make, steps, sign, wait=()):
        out = {}
        for k in steps:
            held = [self.far[-self.width]] if len(self.far) >= self.width else []
            out[k] = self.permute(make(k, [*held, *wait]), k, sign)
            self.far.append(out[k])
        return out

    def send_near(self, make, steps, sign, begin):
        return {
            k: self.permute(make(k, self.far[: begin + j][-1:]), k, sign) for j, k in enumerate(steps)
        }


def local(density, momentum, energy, wall_operator, span_operator, damping, *, chunks):
    jl, zl, nx = density.shape
    ny, nz = wall_operator.shape[0], span_operator.shape[0]
    m, n = lax.axis_size("gy"), lax.axis_size("gz")
    gy, gz = lax.axis_index("gy"), lax.axis_index("gz")
    share = jl // n
    chunks = divisor_up_to(share, chunks)
    rows = share // chunks

    span_to = [jnp.asarray(hop(gz, k, n, 1), jnp.int32).reshape(1) for k in range(n)]
    wall_to = jnp.concatenate([jnp.asarray(hop(gy, k, m, 1), jnp.int32).reshape(1) for k in range(m)])
    wall_from = jnp.concatenate([jnp.asarray(hop(gy, k, m, -1), jnp.int32).reshape(1) for k in range(m)])
    span_from = jnp.concatenate([jnp.asarray(hop(gz, k, n, -1), jnp.int32).reshape(1) for k in range(n)])
    by_share = (
        density.reshape(n, share, zl, nx),
        momentum.reshape(3, n, share, zl, nx),
        energy.reshape(n, share, zl, nx),
    )
    far, near = list(range(n // 2, n))[::-1], list(range(1, n // 2))
    count = len(far)
    sender = Sender("gz", n, WIDTH)

    def pack(c):
        return lambda k, wait: pack_span(span_to[k], c, chunks, *by_share, wait=wait)

    def ordered(pieces):
        return [pieces[k] for k in range(n)]

    def wall_exchange(pieces, sign):
        walls = Sender("gy", m, m)
        moved = walls.send_far(lambda k, wait: after(pieces[k], wait), range(1, m), sign)
        return [pieces[0], *[moved[k] for k in range(1, m)]]

    span_out = []
    for c in range(chunks):
        far_out = sender.send_far(pack(c), far, 1)
        near_out = sender.send_near(pack(c), near, 1, c * count + NEAR)
        span_out.append(ordered({0: pack(c)(0, ()), **far_out, **near_out}))
        if c == 0:
            wall_out = wall_exchange(pack_wall(wall_to, density, momentum, energy), 1)

    identity = jnp.eye(nz, dtype=jnp.float32)
    fourth = 6.0 * identity
    for offset, factor in ((1, -4.0), (-1, -4.0), (2, 1.0), (-2, 1.0)):
        fourth = fourth + factor * jnp.roll(identity, offset, 1)

    def in_order_of_arrival(matrix):
        blocks = matrix.reshape(n, zl, n, zl)
        blocks = jnp.take(jnp.take(blocks, span_from, axis=0), span_from, axis=2)
        return blocks.reshape(nz, nz)

    both = jnp.concatenate([in_order_of_arrival(span_operator), in_order_of_arrival(fourth)], axis=1)
    both = jnp.concatenate(split_outside(both), axis=0)
    wall_both = jnp.concatenate(split_outside(wall_operator), axis=0)

    def weights(c):
        return lax.dynamic_slice_in_dim(damping, gy * jl + gz * share + c * rows, rows)

    def back(c):
        pieces = span_terms(c, weights(c), both, span_out[c])
        return pieces, lambda k, wait: after(pieces[k], wait)

    zz = zl // m
    parts = divisor_up_to(zz, 2)
    wall_back = ()
    for part in range(parts):
        begun = []
        wall_back = wall_terms(
            wall_from, wall_both, damping.reshape(ny, 1), wall_out, part, parts, wall_back, begun
        )
    wall_back = wall_exchange(wall_back, -1)

    pieces, make = back(0)
    far_back = sender.send_far(make, far, -1)
    near_back = sender.send_near(make, near, -1, chunks * count + NEAR)
    span_back = [ordered({0: pieces[0], **far_back, **near_back})]
    *fields, mark = base_fields(wall_to, density, momentum, energy, wall_back)
    fields = (
        fields[0].reshape(n, share, zl, nx),
        fields[1].reshape(3, n, share, zl, nx),
        fields[2].reshape(n, share, zl, nx),
    )

    def add(c, group, wait=()):
        order = jnp.concatenate([span_to[k] for k in group])
        *out, mark = add_span(order, c, chunks, fields, [span_back[c][k] for k in group], wait)
        return out, mark

    for c in range(1, chunks):
        pieces, make = back(c)
        far_back = sender.send_far(make, far[:-2], -1)
        far_back |= sender.send_far(make, far[-2:], -1, [mark])
        fields, mark = add(c - 1, [0, *near, *far])
        near_back = sender.send_near(make, near, -1, (chunks + c) * count + NEAR - 0)
        span_back.append(ordered({0: pieces[0], **far_back, **near_back}))
    last = chunks - 1
    groups = [(last, [0, *near]), (last, far[: count // 2]), (last, far[count // 2 :])]
    for c, group in groups:
        if group:
            fields, _ = add(c, group)
    return (
        fields[0].reshape(jl, zl, nx),
        fields[1].reshape(3, jl, zl, nx),
        fields[2].reshape(jl, zl, nx),
    )


def solution(mesh):
    in_specs = (P("gy", "gz", None), P(None, "gy", "gz", None), P("gy", "gz", None), P(), P(), P())
    out_specs = (P("gy", "gz", None), P(None, "gy", "gz", None), P("gy", "gz", None))
    return jax.shard_map(
        functools.partial(local, chunks=2), mesh=mesh, in_specs=in_specs, out_specs=out_specs, check_vma=False
    )
```

```python
import functools

import jax
import jax.numpy as jnp
from jax import lax
from jax.experimental import pallas as pl
from jax.experimental.pallas import tpu as pltpu
from jax.sharding import PartitionSpec as P

gamma_less = 0.4
time_step = 0.1
vmem_bytes = 63 * 1024 * 1024
WIDTH = 99
NEAR = 1


def divisor_up_to(number, limit):
    return max(d for d in range(1, limit + 1) if number % d == 0)


def hop(index, step, size, sign):
    if size & (size - 1) == 0:
        return index ^ step
    return (index + sign * step) % size


def fluxes(fields, direction):
    density, momentum, energy = fields[0], fields[1:4], fields[4]
    inverse = 1.0 / density
    velocity = momentum[direction] * inverse
    square = momentum[0] * momentum[0] + momentum[1] * momentum[1] + momentum[2] * momentum[2]
    pressure = gamma_less * (energy - 0.5 * square * inverse)
    out = [momentum[direction]]
    for column in range(3):
        product = momentum[column] * velocity
        if column == direction:
            product = product + pressure
        out.append(product)
    out.append((energy + pressure) * velocity)
    return out


def halves(value):
    high = value.astype(jnp.bfloat16)
    low = (value - high.astype(jnp.float32)).astype(jnp.bfloat16)
    return high, low


def split_outside(value):
    high = lax.reduce_precision(value, exponent_bits=8, mantissa_bits=7)
    return high.astype(jnp.bfloat16), (value - high).astype(jnp.bfloat16)


def dot(a, b):
    return jnp.dot(a, b, preferred_element_type=jnp.float32)


def call(body, name, order, operands, grid, in_specs, out_specs, out_shape, scratch=(), aliases=None, flops=0, mark=False, wait=()):
    scalars = tuple(order)
    moved = sum(4 * o.size for o in operands) + sum(4 * o.size for o in jax.tree.leaves(out_shape))
    if wait:
        begin = len(scalars) + len(operands)
        plain = body

        def body(*refs):
            plain(*refs[:begin], *refs[begin + len(wait) :])

        operands = [*operands, *wait]
        in_specs = [*in_specs, *[pl.BlockSpec(memory_space=pl.ANY)] * len(wait)]
    inner = body
    if mark:
        place = len(scalars) + len(operands) + len(out_shape)

        def body(*refs):
            inner(*refs[:place], *refs[place + 1 :])
            refs[place][...] = jnp.zeros_like(refs[place])

        out_specs = [*out_specs, pl.BlockSpec((8, 128), lambda *_: (0, 0))]
        out_shape = [*out_shape, jax.ShapeDtypeStruct((8, 128), jnp.float32)]
    return pl.pallas_call(
        body,
        name=name,
        grid_spec=pltpu.PrefetchScalarGridSpec(
            num_scalar_prefetch=len(scalars),
            grid=grid,
            in_specs=in_specs,
            out_specs=out_specs,
            scratch_shapes=list(scratch),
        ),
        out_shape=out_shape,
        input_output_aliases={} if aliases is None else aliases,
        compiler_params=pltpu.CompilerParams(vmem_limit_bytes=vmem_bytes),
        cost_estimate=pl.CostEstimate(flops=flops, bytes_accessed=moved, transcendentals=0),
    )(*scalars, *operands)


def pack_span_kernel(order, density, momentum, energy, piece):
    piece[0] = density[0]
    for column in range(3):
        piece[1 + column] = momentum[column, 0]
    piece[4] = energy[0]


def pack_span(order, chunk, chunks, density, momentum, energy, wait=()):
    _, share, zl, nx = density.shape
    rows = share // chunks
    r = divisor_up_to(rows, 8)
    first = chunk * (rows // r)
    flat = pl.BlockSpec((1, r, zl, nx), lambda i, s: (s[0], first + i, 0, 0))
    return call(
        pack_span_kernel,
        f"pack_span_{chunk}",
        (order,),
        (density, momentum, energy),
        (rows // r,),
        [flat, pl.BlockSpec((3, 1, r, zl, nx), lambda i, s: (0, s[0], first + i, 0, 0)), flat],
        pl.BlockSpec((5, r, zl, nx), lambda i, s: (0, i, 0, 0)),
        jax.ShapeDtypeStruct((5, rows, zl, nx), jnp.float32),
        wait=wait,
    )


def span_kernel(n, weights, both, *refs):
    pieces, outs = refs[:n], refs[n:]
    _, r, zl, nx = pieces[0].shape
    nz = n * zl

    @pl.loop(0, r)
    def _(row):
        weight = weights[pl.program_id(0) * r + row]
        fields = [jnp.concatenate([p[f, row] for p in pieces], axis=0) for f in range(5)]
        for f, flux in enumerate(fluxes(fields, 2)):
            high, low = halves(jnp.concatenate([flux, weight * fields[f]], axis=0))
            total = dot(both[...], high)
            total = total[:nz] + total[nz:] + dot(both[:nz], low)
            for k, out in enumerate(outs):
                out[f, row] = total[k * zl : (k + 1) * zl]


def span_terms(chunk, weights, both, pieces):
    n = len(pieces)
    _, rows, zl, nx = pieces[0].shape
    r = divisor_up_to(rows, 2)
    nz = n * zl
    spec = pl.BlockSpec((5, r, zl, nx), lambda i, s: (0, i, 0, 0))
    return call(
        functools.partial(span_kernel, n),
        f"span_terms_{chunk}",
        (weights,),
        (both, *pieces),
        (rows // r,),
        [pl.BlockSpec(both.shape, lambda i, s: (0, 0))] + [spec] * n,
        [spec] * n,
        [jax.ShapeDtypeStruct(p.shape, jnp.float32) for p in pieces],
        flops=5 * rows * 6 * nz * 2 * nz * nx,
    )


def pack_wall_kernel(zl, order, density, momentum, energy, *refs):
    pieces, narrow = refs[:-1], refs[-1]
    _, zz, rows, nx = pieces[0].shape
    lane = narrow.shape[-1]
    for half in range(nx // lane):
        lanes = slice(half * lane, (half + 1) * lane)
        narrow[half, 0] = density[:, lanes]
        for column in range(3):
            narrow[half, 1 + column] = momentum[column, :, lanes]
        narrow[half, 4] = energy[:, lanes]
    for k, piece in enumerate(pieces):
        for z in range(zz):
            lines = pl.ds(order[k] * zz + z, rows, stride=zl)
            for half in range(nx // lane):
                lanes = slice(half * lane, (half + 1) * lane)
                for f in range(5):
                    piece[f, z, :, lanes] = narrow[half, f, lines, :]


def pack_wall(blocks, density, momentum, energy, wait=()):
    m = blocks.shape[0]
    jl, zl, nx = density.shape
    zz = zl // m
    lane = divisor_up_to(nx, 128)
    rows = divisor_up_to(jl, 32)
    flat = pl.BlockSpec((rows * zl, nx), lambda i, s: (i, 0))
    return call(
        functools.partial(pack_wall_kernel, zl),
        "pack_wall",
        (blocks,),
        (density.reshape(jl * zl, nx), momentum.reshape(3, jl * zl, nx), energy.reshape(jl * zl, nx)),
        (jl // rows,),
        [flat, pl.BlockSpec((3, rows * zl, nx), lambda i, s: (0, i, 0)), flat],
        [pl.BlockSpec((5, zz, rows, nx), lambda i, s: (0, 0, i, 0))] * m,
        [jax.ShapeDtypeStruct((5, zz, jl, nx), jnp.float32)] * m,
        wait=wait,
        scratch=[pltpu.VMEM((nx // lane, 5, rows * zl, lane), jnp.float32)],
    )


def wall_kernel(m, order, both, damping, *refs):
    pieces, outs = refs[:m], refs[-4 - m : -4]
    kept, flux_high, flux_low, summed = refs[-4:]
    jl, nx = pieces[0].shape[2:]
    ny = m * jl
    step = divisor_up_to(jl, 64)
    for f in range(5):
        kept[f, 0:8] = jnp.zeros((8, nx), jnp.float32)
        kept[f, 8 + ny : 16 + ny] = jnp.zeros((8, nx), jnp.float32)
    for k in range(m):

        @pl.loop(0, jl // step)
        def _(i):
            here = pl.ds(pl.multiple_of(i * step, step), step)
            there = pl.multiple_of(order[k] * jl + i * step, step)
            fields = [pieces[k][f, 0, here, :] for f in range(5)]
            for f, flux in enumerate(fluxes(fields, 1)):
                kept[f, pl.ds(there + 8, step), :] = fields[f]
                flux_high[f, pl.ds(there, step), :], flux_low[f, pl.ds(there, step), :] = halves(flux)

    @pl.loop(0, 5)
    def _(f):
        large = dot(both[...], flux_high[f])
        summed[...] = large[:ny] + large[ny:] + dot(both[:ny], flux_low[f])
        part = divisor_up_to(jl, 128)
        for k in range(m):

            @pl.loop(0, jl // part)
            def _(i):
                at = pl.multiple_of(i * part, part)
                there = pl.multiple_of(order[k] * jl + at, part)
                c = kept[f, pl.ds(there, part + 16), :]

                def shifted(offset):
                    return c[8 + offset : 8 + offset + part]

                fourth = (
                    shifted(-2) - 4.0 * shifted(-1) + 6.0 * shifted(0) - 4.0 * shifted(1) + shifted(2)
                )
                rows = pl.ds(there, part)
                outs[k][f, 0, pl.ds(at, part), :] = summed[rows, :] + damping[rows, :] * fourth


def wall_terms(blocks, both, damping, pieces, part, parts, made=(), wait=()):
    m = len(pieces)
    _, zz, jl, nx = pieces[0].shape
    ny = m * jl
    steps = zz // parts
    spec = pl.BlockSpec((5, 1, jl, nx), lambda i, s: (0, part * steps + i, 0, 0))
    return call(
        functools.partial(wall_kernel, m),
        f"wall_terms_{part}",
        (blocks,),
        (both, damping, *pieces, *made),
        (steps,),
        [pl.BlockSpec((2 * ny, ny), lambda i, s: (0, 0)), pl.BlockSpec((ny, 1), lambda i, s: (0, 0))]
        + [spec] * m
        + [pl.BlockSpec(memory_space=pl.ANY)] * len(made),
        [spec] * m,
        [jax.ShapeDtypeStruct(p.shape, jnp.float32) for p in pieces],
        scratch=[
            pltpu.VMEM((5, ny + 16, nx), jnp.float32),
            pltpu.VMEM((5, ny, nx), jnp.bfloat16),
            pltpu.VMEM((5, ny, nx), jnp.bfloat16),
            pltpu.VMEM((ny, nx), jnp.float32),
        ],
        aliases={3 + m + k: k for k in range(m)} if made else None,
        wait=wait,
        flops=6 * 5 * steps * ny * ny * nx,
    )


def base_kernel(m, zl, order, density, momentum, energy, *refs):
    pieces, outs, wall = refs[:m], refs[m : m + 3], refs[m + 3]
    _, zz, rows, nx = pieces[0].shape
    lane = wall.shape[-1]
    for k, piece in enumerate(pieces):
        for z in range(zz):
            lines = pl.ds(order[k] * zz + z, rows, stride=zl)
            for half in range(nx // lane):
                lanes = slice(half * lane, (half + 1) * lane)
                for f in range(5):
                    wall[half, f, lines, :] = piece[f, z, :, lanes]
    part = divisor_up_to(rows * zl, 64)

    @pl.loop(0, rows * zl // part)
    def _(i):
        here = pl.ds(pl.multiple_of(i * part, part), part)
        fields = [density[here, :]] + [momentum[column, here, :] for column in range(3)] + [energy[here, :]]
        column = lax.broadcasted_iota(jnp.int32, (part, nx), 1)
        for f, flux in enumerate(fluxes(fields, 0)):
            first, last = flux[:, :1], flux[:, nx - 1 :]
            above1 = jnp.where(column >= nx - 1, last, pltpu.roll(flux, nx - 1, 1))
            above2 = jnp.where(column >= nx - 2, last, pltpu.roll(flux, nx - 2, 1))
            below1 = jnp.where(column < 1, first, pltpu.roll(flux, 1, 1))
            below2 = jnp.where(column < 2, first, pltpu.roll(flux, 2, 1))
            along = (8.0 * (above1 - below1) - (above2 - below2)) * (1.0 / 12.0)
            across = jnp.concatenate([wall[half, f, here, :] for half in range(wall.shape[0])], axis=1)
            value = fields[f] - time_step * (along + across)
            if f == 0:
                outs[0][here, :] = value
            elif f == 4:
                outs[2][here, :] = value
            else:
                outs[1][f - 1, here, :] = value


def base_fields(blocks, density, momentum, energy, pieces, wait=()):
    m = len(pieces)
    jl, zl, nx = density.shape
    zz = zl // m
    lane = divisor_up_to(nx, 128)
    rows = divisor_up_to(jl, 16)
    flat = pl.BlockSpec((rows * zl, nx), lambda i, s: (i, 0))
    three = pl.BlockSpec((3, rows * zl, nx), lambda i, s: (0, i, 0))
    shape = jax.ShapeDtypeStruct((jl * zl, nx), jnp.float32)
    outs = call(
        functools.partial(base_kernel, m, zl),
        "base_fields",
        (blocks,),
        (density.reshape(jl * zl, nx), momentum.reshape(3, jl * zl, nx), energy.reshape(jl * zl, nx), *pieces),
        (jl // rows,),
        [flat, three, flat] + [pl.BlockSpec((5, zz, rows, nx), lambda i, s: (0, 0, i, 0))] * m,
        [flat, three, flat],
        [shape, jax.ShapeDtypeStruct((3, jl * zl, nx), jnp.float32), shape],
        scratch=[pltpu.VMEM((nx // lane, 5, rows * zl, lane), jnp.float32)],
        mark=True,
        wait=wait,
    )
    return outs


def add_span_kernel(order, density, momentum, energy, *refs):
    pieces, outs = refs[:-3], refs[-3:]
    for k, piece in enumerate(pieces):

        @pl.when(pl.program_id(0) == k)
        def _():
            outs[0][0] = density[0] - time_step * piece[0]
            for column in range(3):
                outs[1][column, 0] = momentum[column, 0] - time_step * piece[1 + column]
            outs[2][0] = energy[0] - time_step * piece[4]


def add_span(order, chunk, chunks, fields, pieces, wait=()):
    share, zl, nx = fields[0].shape[1:]
    rows = share // chunks
    r = divisor_up_to(rows, 8)
    steps = rows // r
    first = chunk * steps
    flat = pl.BlockSpec((1, r, zl, nx), lambda p, i, s: (s[p], first + i, 0, 0))
    three = pl.BlockSpec((3, 1, r, zl, nx), lambda p, i, s: (0, s[p], first + i, 0, 0))

    def own(k):
        def index(p, i, s):
            return 0, jnp.where(p == k, i, jnp.where(p < k, 0, steps - 1)), 0, 0

        return pl.BlockSpec((5, r, zl, nx), index)

    return call(
        add_span_kernel,
        f"add_span_{chunk}",
        (order,),
        (*fields, *pieces),
        (len(pieces), steps),
        [flat, three, flat] + [own(k) for k in range(len(pieces))],
        [flat, three, flat],
        [jax.ShapeDtypeStruct(f.shape, f.dtype) for f in fields],
        aliases={1: 0, 2: 1, 3: 2},
        mark=True,
        wait=wait,
    )


def after(value, wait):
    if not wait:
        return value
    anywhere = pl.BlockSpec(memory_space=pl.ANY)
    return pl.pallas_call(
        lambda *refs: None,
        name="after",
        in_specs=[anywhere] * (1 + len(wait)),
        out_specs=anywhere,
        out_shape=jax.ShapeDtypeStruct(value.shape, value.dtype),
        input_output_aliases={0: 0},
        compiler_params=pltpu.CompilerParams(vmem_limit_bytes=vmem_bytes),
        cost_estimate=pl.CostEstimate(flops=0, bytes_accessed=0, transcendentals=0),
    )(value, *wait)


class Sender:
    def __init__(self, axis, size, width):
        self.axis, self.size, self.width, self.far = axis, size, width, []

    def permute(self, piece, step, sign):
        pairs = [(i, hop(i, step, self.size, sign)) for i in range(self.size)]
        return lax.ppermute(piece, self.axis, pairs)

    def send_far(self, make, steps, sign, wait=()):
        out = {}
        for k in steps:
            held = [self.far[-self.width]] if len(self.far) >= self.width else []
            out[k] = self.permute(make(k, [*held, *wait]), k, sign)
            self.far.append(out[k])
        return out

    def send_near(self, make, steps, sign, begin):
        return {
            k: self.permute(make(k, self.far[: begin + j][-1:]), k, sign) for j, k in enumerate(steps)
        }


def local(density, momentum, energy, wall_operator, span_operator, damping, *, chunks):
    jl, zl, nx = density.shape
    ny, nz = wall_operator.shape[0], span_operator.shape[0]
    m, n = lax.axis_size("gy"), lax.axis_size("gz")
    gy, gz = lax.axis_index("gy"), lax.axis_index("gz")
    share = jl // n
    chunks = divisor_up_to(share, chunks)
    rows = share // chunks

    span_to = [jnp.asarray(hop(gz, k, n, 1), jnp.int32).reshape(1) for k in range(n)]
    wall_to = jnp.concatenate([jnp.asarray(hop(gy, k, m, 1), jnp.int32).reshape(1) for k in range(m)])
    wall_from = jnp.concatenate([jnp.asarray(hop(gy, k, m, -1), jnp.int32).reshape(1) for k in range(m)])
    span_from = jnp.concatenate([jnp.asarray(hop(gz, k, n, -1), jnp.int32).reshape(1) for k in range(n)])
    by_share = (
        density.reshape(n, share, zl, nx),
        momentum.reshape(3, n, share, zl, nx),
        energy.reshape(n, share, zl, nx),
    )
    far, near = list(range(n // 2, n))[::-1], list(range(1, n // 2))
    count = len(far)
    sender = Sender("gz", n, WIDTH)

    def pack(c):
        return lambda k, wait: pack_span(span_to[k], c, chunks, *by_share, wait=wait)

    def ordered(pieces):
        return [pieces[k] for k in range(n)]

    def wall_exchange(pieces, sign):
        walls = Sender("gy", m, m)
        moved = walls.send_far(lambda k, wait: after(pieces[k], wait), range(1, m), sign)
        return [pieces[0], *[moved[k] for k in range(1, m)]]

    span_out = []
    for c in range(chunks):
        far_out = sender.send_far(pack(c), far, 1)
        near_out = sender.send_near(pack(c), near, 1, c * count + NEAR)
        span_out.append(ordered({0: pack(c)(0, ()), **far_out, **near_out}))
        if c == 0:
            begun = [far_out[far[0]]]
            wall_out = wall_exchange(pack_wall(wall_to, density, momentum, energy, begun), 1)

    identity = jnp.eye(nz, dtype=jnp.float32)
    fourth = 6.0 * identity
    for offset, factor in ((1, -4.0), (-1, -4.0), (2, 1.0), (-2, 1.0)):
        fourth = fourth + factor * jnp.roll(identity, offset, 1)

    def in_order_of_arrival(matrix):
        blocks = matrix.reshape(n, zl, n, zl)
        blocks = jnp.take(jnp.take(blocks, span_from, axis=0), span_from, axis=2)
        return blocks.reshape(nz, nz)

    both = jnp.concatenate([in_order_of_arrival(span_operator), in_order_of_arrival(fourth)], axis=1)
    both = jnp.concatenate(split_outside(both), axis=0)
    wall_both = jnp.concatenate(split_outside(wall_operator), axis=0)

    def weights(c):
        return lax.dynamic_slice_in_dim(damping, gy * jl + gz * share + c * rows, rows)

    def back(c):
        pieces = span_terms(c, weights(c), both, span_out[c])
        return pieces, lambda k, wait: after(pieces[k], wait)

    zz = zl // m
    parts = divisor_up_to(zz, 2)
    wall_back = ()
    for part in range(parts):
        begun = []
        wall_back = wall_terms(
            wall_from, wall_both, damping.reshape(ny, 1), wall_out, part, parts, wall_back, begun
        )
    wall_back = wall_exchange(wall_back, -1)

    pieces, make = back(0)
    far_back = sender.send_far(make, far, -1)
    near_back = sender.send_near(make, near, -1, chunks * count + NEAR)
    span_back = [ordered({0: pieces[0], **far_back, **near_back})]
    *fields, mark = base_fields(wall_to, density, momentum, energy, wall_back)
    fields = (
        fields[0].reshape(n, share, zl, nx),
        fields[1].reshape(3, n, share, zl, nx),
        fields[2].reshape(n, share, zl, nx),
    )

    def add(c, group, wait=()):
        order = jnp.concatenate([span_to[k] for k in group])
        *out, mark = add_span(order, c, chunks, fields, [span_back[c][k] for k in group], wait)
        return out, mark

    for c in range(1, chunks):
        pieces, make = back(c)
        far_back = sender.send_far(make, far, -1)
        near_back = sender.send_near(make, near, -1, (chunks + c) * count + NEAR)
        span_back.append(ordered({0: pieces[0], **far_back, **near_back}))
    last = chunks - 1
    groups = [(c, [0, *near, *far]) for c in range(last)]
    groups += [(last, [0, *near]), (last, far[: count // 2]), (last, far[count // 2 :])]
    for c, group in groups:
        if group:
            fields, _ = add(c, group)
    return (
        fields[0].reshape(jl, zl, nx),
        fields[1].reshape(3, jl, zl, nx),
        fields[2].reshape(jl, zl, nx),
    )


def solution(mesh):
    in_specs = (P("gy", "gz", None), P(None, "gy", "gz", None), P("gy", "gz", None), P(), P(), P())
    out_specs = (P("gy", "gz", None), P(None, "gy", "gz", None), P("gy", "gz", None))
    return jax.shard_map(
        functools.partial(local, chunks=2), mesh=mesh, in_specs=in_specs, out_specs=out_specs, check_vma=False
    )
```

```python
import functools

import jax
import jax.numpy as jnp
from jax import lax
from jax.experimental import pallas as pl
from jax.experimental.pallas import tpu as pltpu
from jax.sharding import PartitionSpec as P

gamma_less = 0.4
time_step = 0.1
vmem_bytes = 56 * 1024 * 1024


def divisor_up_to(number, limit):
    return max(d for d in range(1, limit + 1) if number % d == 0)


def hop(index, step, size, sign):
    if size & (size - 1) == 0:
        return index ^ step
    return (index + sign * step) % size


def fluxes(fields, direction):
    density, momentum, energy = fields[0], fields[1:4], fields[4]
    inverse = 1.0 / density
    velocity = momentum[direction] * inverse
    square = momentum[0] * momentum[0] + momentum[1] * momentum[1] + momentum[2] * momentum[2]
    pressure = gamma_less * (energy - 0.5 * square * inverse)
    out = [momentum[direction]]
    for column in range(3):
        product = momentum[column] * velocity
        if column == direction:
            product = product + pressure
        out.append(product)
    out.append((energy + pressure) * velocity)
    return out


def halves(value):
    high = value.astype(jnp.bfloat16)
    low = (value - high.astype(jnp.float32)).astype(jnp.bfloat16)
    return high, low


def split_outside(value):
    high = lax.reduce_precision(value, exponent_bits=8, mantissa_bits=7)
    return high.astype(jnp.bfloat16), (value - high).astype(jnp.bfloat16)


def dot(a, b):
    return jnp.dot(a, b, preferred_element_type=jnp.float32)


def call(body, name, order, operands, grid, in_specs, out_specs, out_shape, scratch=(), aliases=None, flops=0):
    scalars = tuple(order)
    moved = sum(4 * o.size for o in operands) + sum(4 * o.size for o in out_shape)
    return pl.pallas_call(
        body,
        name=name,
        grid_spec=pltpu.PrefetchScalarGridSpec(
            num_scalar_prefetch=len(scalars),
            grid=grid,
            in_specs=in_specs,
            out_specs=out_specs,
            scratch_shapes=list(scratch),
        ),
        out_shape=out_shape,
        input_output_aliases={} if aliases is None else aliases,
        compiler_params=pltpu.CompilerParams(vmem_limit_bytes=vmem_bytes),
        cost_estimate=pl.CostEstimate(flops=flops, bytes_accessed=moved, transcendentals=0),
    )(*scalars, *operands)


def pack_span_kernel(order, density, momentum, energy, *pieces):
    for k, piece in enumerate(pieces):
        block = order[k]
        piece[0] = density[block]
        for column in range(3):
            piece[1 + column] = momentum[column, block]
        piece[4] = energy[block]


def pack_span(blocks, chunk, chunks, density, momentum, energy):
    n, share, zl, nx = density.shape
    rows = share // chunks
    r = divisor_up_to(rows, 2)
    first = chunk * (rows // r)
    flat = pl.BlockSpec((n, r, zl, nx), lambda i, s: (0, first + i, 0, 0))
    return call(
        pack_span_kernel,
        f"pack_span_{chunk}",
        (blocks,),
        (density, momentum, energy),
        (rows // r,),
        [flat, pl.BlockSpec((3, n, r, zl, nx), lambda i, s: (0, 0, first + i, 0, 0)), flat],
        [pl.BlockSpec((5, r, zl, nx), lambda i, s: (0, i, 0, 0))] * n,
        [jax.ShapeDtypeStruct((5, rows, zl, nx), jnp.float32)] * n,
    )


def span_kernel(n, weights, both, *refs):
    pieces, outs = refs[:n], refs[n:]
    _, r, zl, nx = pieces[0].shape
    nz = n * zl

    @pl.loop(0, r)
    def _(row):
        weight = weights[pl.program_id(0) * r + row]
        fields = [jnp.concatenate([p[f, row] for p in pieces], axis=0) for f in range(5)]
        for f, flux in enumerate(fluxes(fields, 2)):
            high, low = halves(jnp.concatenate([flux, weight * fields[f]], axis=0))
            total = dot(both[...], high)
            total = total[:nz] + total[nz:] + dot(both[:nz], low)
            for k, out in enumerate(outs):
                out[f, row] = total[k * zl : (k + 1) * zl]


def span_terms(chunk, weights, both, pieces):
    n = len(pieces)
    _, rows, zl, nx = pieces[0].shape
    r = divisor_up_to(rows, 2)
    nz = n * zl
    spec = pl.BlockSpec((5, r, zl, nx), lambda i, s: (0, i, 0, 0))
    return call(
        functools.partial(span_kernel, n),
        f"span_terms_{chunk}",
        (weights,),
        (both, *pieces),
        (rows // r,),
        [pl.BlockSpec(both.shape, lambda i, s: (0, 0))] + [spec] * n,
        [spec] * n,
        [jax.ShapeDtypeStruct(p.shape, jnp.float32) for p in pieces],
        flops=5 * rows * 6 * nz * 2 * nz * nx,
    )


def pack_wall_kernel(zl, order, density, momentum, energy, *refs):
    pieces, narrow = refs[:-1], refs[-1]
    _, zz, rows, nx = pieces[0].shape
    lane = narrow.shape[-1]
    for half in range(nx // lane):
        lanes = slice(half * lane, (half + 1) * lane)
        narrow[half, 0] = density[:, lanes]
        for column in range(3):
            narrow[half, 1 + column] = momentum[column, :, lanes]
        narrow[half, 4] = energy[:, lanes]
    for k, piece in enumerate(pieces):
        for z in range(zz):
            lines = pl.ds(order[k] * zz + z, rows, stride=zl)
            for half in range(nx // lane):
                lanes = slice(half * lane, (half + 1) * lane)
                for f in range(5):
                    piece[f, z, :, lanes] = narrow[half, f, lines, :]


def pack_wall(blocks, density, momentum, energy):
    m = blocks.shape[0]
    jl, zl, nx = density.shape
    zz = zl // m
    lane = divisor_up_to(nx, 128)
    rows = divisor_up_to(jl, 32)
    flat = pl.BlockSpec((rows * zl, nx), lambda i, s: (i, 0))
    return call(
        functools.partial(pack_wall_kernel, zl),
        "pack_wall",
        (blocks,),
        (density.reshape(jl * zl, nx), momentum.reshape(3, jl * zl, nx), energy.reshape(jl * zl, nx)),
        (jl // rows,),
        [flat, pl.BlockSpec((3, rows * zl, nx), lambda i, s: (0, i, 0)), flat],
        [pl.BlockSpec((5, zz, rows, nx), lambda i, s: (0, 0, i, 0))] * m,
        [jax.ShapeDtypeStruct((5, zz, jl, nx), jnp.float32)] * m,
        scratch=[pltpu.VMEM((nx // lane, 5, rows * zl, lane), jnp.float32)],
    )


def wall_kernel(m, order, high, low, damping, *refs):
    pieces, outs = refs[:m], refs[m : 2 * m]
    kept, flux_high, flux_low = refs[2 * m :]
    jl, nx = pieces[0].shape[2:]
    ny = m * jl
    step = divisor_up_to(jl, 64)
    for f in range(5):
        kept[f, 0:8] = jnp.zeros((8, nx), jnp.float32)
        kept[f, 8 + ny : 16 + ny] = jnp.zeros((8, nx), jnp.float32)
    for k in range(m):

        @pl.loop(0, jl // step)
        def _(i):
            here = pl.ds(pl.multiple_of(i * step, step), step)
            there = pl.multiple_of(order[k] * jl + i * step, step)
            fields = [pieces[k][f, 0, here, :] for f in range(5)]
            for f, flux in enumerate(fluxes(fields, 1)):
                kept[f, pl.ds(there + 8, step), :] = fields[f]
                flux_high[f, pl.ds(there, step), :], flux_low[f, pl.ds(there, step), :] = halves(flux)

    for k in range(m):
        first = pl.multiple_of(order[k] * jl, jl)
        rows = pl.ds(first, jl)

        @pl.loop(0, 5)
        def _(f):
            total = dot(high[rows, :], flux_high[f]) + dot(low[rows, :], flux_high[f])
            outs[k][f, 0] = total + dot(high[rows, :], flux_low[f])
            part = divisor_up_to(jl, 128)

            @pl.loop(0, jl // part)
            def _(i):
                at = pl.multiple_of(i * part, part)
                c = kept[f, pl.ds(first + at, part + 16), :]

                def shifted(offset):
                    return c[8 + offset : 8 + offset + part]

                fourth = (
                    shifted(-2) - 4.0 * shifted(-1) + 6.0 * shifted(0) - 4.0 * shifted(1) + shifted(2)
                )
                weight = damping[pl.ds(first + at, part), :]
                outs[k][f, 0, pl.ds(at, part), :] += weight * fourth


def wall_terms(blocks, operator, damping, pieces):
    m = len(pieces)
    _, zz, jl, nx = pieces[0].shape
    ny = m * jl
    high, low = split_outside(operator)
    spec = pl.BlockSpec((5, 1, jl, nx), lambda i, s: (0, i, 0, 0))
    whole = pl.BlockSpec((ny, ny), lambda i, s: (0, 0))
    return call(
        functools.partial(wall_kernel, m),
        "wall_terms",
        (blocks,),
        (high, low, damping.reshape(ny, 1), *pieces),
        (zz,),
        [whole, whole, pl.BlockSpec((ny, 1), lambda i, s: (0, 0))] + [spec] * m,
        [spec] * m,
        [jax.ShapeDtypeStruct(p.shape, jnp.float32) for p in pieces],
        scratch=[
            pltpu.VMEM((5, ny + 16, nx), jnp.float32),
            pltpu.VMEM((5, ny, nx), jnp.bfloat16),
            pltpu.VMEM((5, ny, nx), jnp.bfloat16),
        ],
        flops=6 * 5 * zz * ny * ny * nx,
    )


def base_kernel(m, zl, order, density, momentum, energy, *refs):
    pieces, outs, wall = refs[:m], refs[m : m + 3], refs[m + 3]
    _, zz, rows, nx = pieces[0].shape
    lane = wall.shape[-1]
    for k, piece in enumerate(pieces):
        for z in range(zz):
            lines = pl.ds(order[k] * zz + z, rows, stride=zl)
            for half in range(nx // lane):
                lanes = slice(half * lane, (half + 1) * lane)
                for f in range(5):
                    wall[half, f, lines, :] = piece[f, z, :, lanes]
    part = divisor_up_to(rows * zl, 64)

    @pl.loop(0, rows * zl // part)
    def _(i):
        here = pl.ds(pl.multiple_of(i * part, part), part)
        fields = [density[here, :]] + [momentum[column, here, :] for column in range(3)] + [energy[here, :]]
        column = lax.broadcasted_iota(jnp.int32, (part, nx), 1)
        for f, flux in enumerate(fluxes(fields, 0)):
            first, last = flux[:, :1], flux[:, nx - 1 :]
            above1 = jnp.where(column >= nx - 1, last, pltpu.roll(flux, nx - 1, 1))
            above2 = jnp.where(column >= nx - 2, last, pltpu.roll(flux, nx - 2, 1))
            below1 = jnp.where(column < 1, first, pltpu.roll(flux, 1, 1))
            below2 = jnp.where(column < 2, first, pltpu.roll(flux, 2, 1))
            along = (8.0 * (above1 - below1) - (above2 - below2)) * (1.0 / 12.0)
            across = jnp.concatenate([wall[half, f, here, :] for half in range(wall.shape[0])], axis=1)
            value = fields[f] - time_step * (along + across)
            if f == 0:
                outs[0][here, :] = value
            elif f == 4:
                outs[2][here, :] = value
            else:
                outs[1][f - 1, here, :] = value


def base_fields(blocks, density, momentum, energy, pieces):
    m = len(pieces)
    jl, zl, nx = density.shape
    zz = zl // m
    lane = divisor_up_to(nx, 128)
    rows = divisor_up_to(jl, 16)
    flat = pl.BlockSpec((rows * zl, nx), lambda i, s: (i, 0))
    three = pl.BlockSpec((3, rows * zl, nx), lambda i, s: (0, i, 0))
    shape = jax.ShapeDtypeStruct((jl * zl, nx), jnp.float32)
    outs = call(
        functools.partial(base_kernel, m, zl),
        "base_fields",
        (blocks,),
        (density.reshape(jl * zl, nx), momentum.reshape(3, jl * zl, nx), energy.reshape(jl * zl, nx), *pieces),
        (jl // rows,),
        [flat, three, flat] + [pl.BlockSpec((5, zz, rows, nx), lambda i, s: (0, 0, i, 0))] * m,
        [flat, three, flat],
        [shape, jax.ShapeDtypeStruct((3, jl * zl, nx), jnp.float32), shape],
        scratch=[pltpu.VMEM((nx // lane, 5, rows * zl, lane), jnp.float32)],
    )
    return outs


def add_span_kernel(n, order, density, momentum, energy, *refs):
    pieces, outs = refs[:n], refs[n:]
    for k, piece in enumerate(pieces):
        block = order[k]
        outs[0][block] = density[block] - time_step * piece[0]
        for column in range(3):
            outs[1][column, block] = momentum[column, block] - time_step * piece[1 + column]
        outs[2][block] = energy[block] - time_step * piece[4]


def add_span(blocks, chunk, chunks, fields, pieces):
    n = len(pieces)
    share, zl, nx = fields[0].shape[1:]
    rows = share // chunks
    r = divisor_up_to(rows, 2)
    first = chunk * (rows // r)
    flat = pl.BlockSpec((n, r, zl, nx), lambda i, s: (0, first + i, 0, 0))
    three = pl.BlockSpec((3, n, r, zl, nx), lambda i, s: (0, 0, first + i, 0, 0))
    return call(
        functools.partial(add_span_kernel, n),
        f"add_span_{chunk}",
        (blocks,),
        (*fields, *pieces),
        (rows // r,),
        [flat, three, flat] + [pl.BlockSpec((5, r, zl, nx), lambda i, s: (0, i, 0, 0))] * n,
        [flat, three, flat],
        [jax.ShapeDtypeStruct(f.shape, f.dtype) for f in fields],
        aliases={1: 0, 2: 1, 3: 2},
    )


def exchange(pieces, axis, sign, sequence):
    size = len(pieces)
    out = list(pieces)
    for k in sequence:
        pairs = [(i, hop(i, k, size, sign)) for i in range(size)]
        out[k] = lax.ppermute(pieces[k], axis, pairs)
    return out


def local(density, momentum, energy, wall_operator, span_operator, damping, *, chunks):
    jl, zl, nx = density.shape
    nz = span_operator.shape[0]
    m, n = lax.axis_size("gy"), lax.axis_size("gz")
    gy, gz = lax.axis_index("gy"), lax.axis_index("gz")
    share = jl // n
    chunks = divisor_up_to(share, chunks)
    rows = share // chunks

    span_to = jnp.stack([jnp.asarray(hop(gz, k, n, 1), jnp.int32) for k in range(n)])
    span_from = jnp.stack([jnp.asarray(hop(gz, k, n, -1), jnp.int32) for k in range(n)])
    wall_to = jnp.stack([jnp.asarray(hop(gy, k, m, 1), jnp.int32) for k in range(m)])
    wall_from = jnp.stack([jnp.asarray(hop(gy, k, m, -1), jnp.int32) for k in range(m)])

    by_share = (
        density.reshape(n, share, zl, nx),
        momentum.reshape(3, n, share, zl, nx),
        energy.reshape(n, share, zl, nx),
    )
    far_first = range(n - 1, 0, -1)
    span_out = [
        exchange(pack_span(span_to, c, chunks, *by_share), "gz", 1, far_first) for c in range(chunks)
    ]
    wall_out = exchange(pack_wall(wall_to, density, momentum, energy), "gy", 1, range(m - 1, 0, -1))

    identity = jnp.eye(nz, dtype=jnp.float32)
    fourth = 6.0 * identity
    for offset, factor in ((1, -4.0), (-1, -4.0), (2, 1.0), (-2, 1.0)):
        fourth = fourth + factor * jnp.roll(identity, offset, 1)

    def in_order_of_arrival(matrix):
        blocks = matrix.reshape(n, zl, n, zl)
        blocks = jnp.take(jnp.take(blocks, span_from, axis=0), span_from, axis=2)
        return blocks.reshape(nz, nz)

    both = jnp.concatenate([in_order_of_arrival(span_operator), in_order_of_arrival(fourth)], axis=1)
    both = jnp.concatenate(split_outside(both), axis=0)

    wall_back = exchange(wall_terms(wall_from, wall_operator, damping, wall_out), "gy", -1, range(m - 1, 0, -1))
    span_back = []
    for c in range(chunks):
        weights = lax.dynamic_slice_in_dim(damping, gy * jl + gz * share + c * rows, rows)
        span_back.append(exchange(span_terms(c, weights, both, span_out[c]), "gz", -1, far_first))

    fields = base_fields(wall_to, density, momentum, energy, wall_back)
    fields = (
        fields[0].reshape(n, share, zl, nx),
        fields[1].reshape(3, n, share, zl, nx),
        fields[2].reshape(n, share, zl, nx),
    )
    for c in range(chunks):
        fields = add_span(span_to, c, chunks, fields, span_back[c])
    return (
        fields[0].reshape(jl, zl, nx),
        fields[1].reshape(3, jl, zl, nx),
        fields[2].reshape(jl, zl, nx),
    )


def solution(mesh):
    in_specs = (P("gy", "gz", None), P(None, "gy", "gz", None), P("gy", "gz", None), P(), P(), P())
    out_specs = (P("gy", "gz", None), P(None, "gy", "gz", None), P("gy", "gz", None))
    return jax.shard_map(
        functools.partial(local, chunks=2), mesh=mesh, in_specs=in_specs, out_specs=out_specs, check_vma=False
    )
```
